32 devices in a mesh: ctx: 4 (over y, core), db: 4 (over z), tp: 2 (over x).
Axes of the slice: x: 2, y: 2, z: 4, core: 2. Of those that a mesh axis runs over, the one named last changes fastest.
Arguments:
- hidden_in: bfloat16 [4, 1024, 4096], P('db', 'ctx', 'tp'), may hold values from -6 to 6
- queries: bfloat16 [4, 1024, 4096], P('db', 'ctx', 'tp')
- keys: bfloat16 [4, 1024, 4096], P('db', 'ctx', 'tp')
- values: bfloat16 [4, 1024, 4096], P('db', 'ctx', 'tp'), may hold values from -6 to 6
- cross_queries: bfloat16 [4, 1024, 4096], P('db', 'ctx', 'tp')
- neighbours: int32 [4, 16, 2], P('db', 'ctx'), may hold values from 0 to 31, as said below
- database: bfloat16 [2, 32, 128, 4096], P(None, 'db', None, 'tp')
- out_weight: bfloat16 [4096, 4096], P('tp', 'db'), may hold values from -0.125 to 0.125
Outputs:
- attended: bfloat16 [4, 1024, 4096], P('db', 'ctx', 'tp')
- mixed: bfloat16 [4, 1024, 4096], P('db', 'ctx', 'tp')
The draws below stay inside these ranges and needn't reach their ends.
Inputs may be any that keep to these rules, and one draw needn't show every extreme that they name: `neighbours`: block id n is held by database shard n // 8. Among the 8 entries of the retrieval blocks of each aligned run of 256 positions of a sequence, no shard holds more than 4, and one shard holds exactly 4; in each such run of positions this shard is the same for all sequences.
All inputs are finite; a program needn't handle non-finite values.
Results may differ from the reference program's by a relative error of at most 0.007.
Values may be sent and summed in bfloat16 or wider, within the bound.
No kernel may reach another device: no remote copies, remote signals or barrier semaphores. Data moves between devices by JAX's collectives and lax.ppermute only.
A program may use at most 128 MiB of HBM per device.

```python
import jax
import jax.numpy as jnp
from jax import lax

D = 4096
HEADS = 32
DH = 128
TOK_DEV = 256
SPAN = 64
NEIGH = 2
NB_LEN = 128
SEQS = 4
LEN = 1024
SPANS = 16
LOOKUPS = 8
MOST = 4
DB_DEV = 8
DB_BLOCKS = 32
N_TP = 2


def pick_neighbours(key):
    base = jax.random.fold_in(key, 301)
    run_count = LEN // TOK_DEV
    hot_owner = jax.random.randint(jax.random.fold_in(base, 1), (run_count,), 0, SEQS)
    offset = jax.random.randint(jax.random.fold_in(base, 2), (SEQS, run_count, LOOKUPS), 1, SEQS)
    slot_index = jnp.arange(LOOKUPS, dtype=jnp.int32)
    owners = jnp.where(slot_index[None, None, :] < MOST, hot_owner[None, :, None], (hot_owner[None, :, None] + offset) % SEQS)
    ranking = jax.random.randint(jax.random.fold_in(base, 3), (SEQS, run_count, LOOKUPS), 0, 2 ** 20) * LOOKUPS + slot_index
    order = jnp.argsort(ranking, axis=-1)
    owners = jnp.take_along_axis(owners, order, axis=-1)
    local_ids = jax.random.randint(jax.random.fold_in(base, 4), (SEQS, run_count, LOOKUPS), 0, DB_DEV)
    return (owners * DB_DEV + local_ids).reshape(SEQS, SPANS, NEIGH).astype(jnp.int32)


def database_keys(key):
    return jax.random.normal(jax.random.fold_in(key, 201), (DB_BLOCKS, NB_LEN, D), jnp.float32)


def self_keys(key):
    return jax.random.normal(jax.random.fold_in(key, 101), (SEQS, LEN, D), jnp.float32)


def draw_neighbours(key, part):
    return pick_neighbours(key)


def draw_database(key, part):
    key_rows = database_keys(key)
    value_rows = jax.random.normal(jax.random.fold_in(key, 202), (DB_BLOCKS, NB_LEN, D), jnp.float32)
    return jnp.stack([key_rows, value_rows]).astype(jnp.bfloat16)


def draw_keys(key, part):
    base_rows = self_keys(key)
    return base_rows.astype(jnp.bfloat16)


def draw_queries(key, part):
    drawn = 2.0 * jax.random.normal(jax.random.fold_in(key, 102), (SEQS, LEN, D), jnp.float32)
    return drawn.astype(jnp.bfloat16)


def draw_cross_queries(key, part):
    drawn = 2.0 * jax.random.normal(jax.random.fold_in(key, 203), (SEQS, LEN, D), jnp.float32)
    return drawn.astype(jnp.bfloat16)


def raised(entries, own_key, source, target, blocks, factor):
    def block_of(dim):
        return (jnp.arange(entries.shape[dim]) // (entries.shape[dim] // blocks)).reshape((-1,) + (1,) * (entries.ndim - 1 - dim))

    one_side = jax.random.permutation(own_key, blocks)[block_of(target)]
    other_side = (block_of(target) + blocks // 2) % blocks
    return jnp.where((block_of(source) == one_side) | (block_of(source) == other_side), factor * entries, entries)


def levels(own_key, shape, pieces, smallest, largest):
    loudness, own = 1.0, jax.random.fold_in(own_key, 6)
    for dim, shards_of in pieces:
        steps = jnp.exp(jax.random.uniform(jax.random.fold_in(own, dim), (shards_of,), jnp.float32, smallest / len(pieces), largest / len(pieces)))
        loudness = loudness * jnp.repeat(steps, shape[dim] // shards_of).reshape([-1 if axis == dim else 1 for axis in range(len(shape))])
    return loudness


def bell_draw(own_key, dims, width, bound, shards=(), kind=jnp.bfloat16):
    result = width * jax.random.normal(own_key, dims, jnp.float32)
    if shards:
        result = result * levels(own_key, dims, shards, -0.22, 0.18)
    return jnp.clip(result, -bound, bound).astype(kind)


def gaussian_with(rng, extent, width, limit, cuts, heavy, kind=jnp.bfloat16):
    values = width * jax.random.normal(rng, extent, jnp.float32)
    if cuts:
        values = values * levels(rng, extent, cuts, -0.22, 0.18)
    return jnp.clip(raised(values, jax.random.fold_in(rng, 3), *heavy), -limit, limit).astype(kind)


def setup_inputs(seed: int = 0) -> dict:
    splits = jax.random.split(jax.random.key(seed), 9)
    hidden_in = bell_draw(splits[0], (SEQS, LEN, D), 1.0, 6.0, ((0, 4), (1, 4), (2, 2)))
    queries = draw_queries(jax.random.fold_in(splits[8], 71), 0)
    keys = draw_keys(jax.random.fold_in(splits[8], 71), 0)
    values = bell_draw(splits[3], (SEQS, LEN, D), 1.0, 6.0, ((0, 4), (1, 4), (2, 2)))
    cross_queries = draw_cross_queries(jax.random.fold_in(splits[8], 71), 0)
    neighbours = draw_neighbours(jax.random.fold_in(splits[8], 71), 0)
    database = draw_database(jax.random.fold_in(splits[8], 71), 0)
    out_weight = gaussian_with(splits[7], (D, D), D ** -0.5, 0.125, ((0, 2), (1, 4)), (0, 1, 4, 2.0))
    return dict(hidden_in=hidden_in, queries=queries, keys=keys, values=values, cross_queries=cross_queries, neighbours=neighbours, database=database, out_weight=out_weight)


def reference(hidden_in, queries, keys, values, cross_queries, neighbours, database, out_weight):
    scale = 1.0 / (DH ** 0.5)

    def by_head(array):
        return array.reshape(SEQS, LEN, HEADS, DH).transpose(0, 2, 1, 3).reshape(SEQS * HEADS, LEN, DH)

    q_all = by_head(queries)
    k_all = by_head(keys)
    v_all = by_head(values)
    position = jnp.arange(LEN, dtype=jnp.int32)
    allowed = position[None, :] <= position[:, None]

    def self_head(item):
        score = jnp.dot(q_all[item], k_all[item].T, preferred_element_type=jnp.float32) * scale
        peak = jnp.max(jnp.where(allowed, score, -1e30), axis=-1)
        weights = jnp.where(allowed, jnp.exp(score - peak[:, None]), 0.0)
        total = jnp.sum(weights, axis=-1)
        accum = jnp.dot(weights.astype(jnp.bfloat16), v_all[item], preferred_element_type=jnp.float32)
        return (accum / total[:, None]).astype(jnp.bfloat16)

    heads_out = lax.map(self_head, jnp.arange(SEQS * HEADS, dtype=jnp.int32))
    attended = heads_out.reshape(SEQS, HEADS, LEN, DH).transpose(0, 2, 1, 3).reshape(SEQS, LEN, D)

    def cross_item(item):
        seq_index = item // SPANS
        span_index = item % SPANS
        query = lax.dynamic_slice_in_dim(cross_queries[seq_index], (span_index * SPAN).astype(jnp.int32), SPAN, 0)
        block_ids = neighbours[seq_index, span_index]
        near_keys = database[0][block_ids].reshape(NEIGH * NB_LEN, HEADS, DH).astype(jnp.float32)
        near_values = database[1][block_ids].reshape(NEIGH * NB_LEN, HEADS, DH).astype(jnp.float32)
        query_heads = query.reshape(SPAN, HEADS, DH).astype(jnp.float32)
        score = jnp.einsum("qhd,khd->hqk", query_heads, near_keys) * scale
        peak = jnp.max(score, axis=-1)
        weights = jnp.exp(score - peak[..., None])
        total = jnp.sum(weights, axis=-1)
        rounded = lax.optimization_barrier(weights.astype(jnp.bfloat16)).astype(jnp.float32)
        accum = jnp.einsum("hqk,khd->qhd", rounded, near_values)
        return (accum / total.T[:, :, None]).reshape(SPAN, D).astype(jnp.bfloat16)

    cross_out = lax.map(cross_item, jnp.arange(SEQS * SPANS, dtype=jnp.int32)).reshape(SEQS * LEN, D)
    rows_block = D // N_TP
    summed = hidden_in.reshape(SEQS * LEN, D).astype(jnp.float32)
    for block in range(N_TP):
        part_sum = jnp.dot(cross_out[:, block * rows_block:(block + 1) * rows_block], out_weight[block * rows_block:(block + 1) * rows_block, :], preferred_element_type=jnp.float32)
        summed = summed + lax.optimization_barrier(part_sum.astype(jnp.bfloat16)).astype(jnp.float32)
    mixed = summed.astype(jnp.bfloat16).reshape(SEQS, LEN, D)
    return attended, mixed
```

```python
import functools
import math

import jax
import jax.numpy as jnp
from jax import lax
from jax.experimental import pallas as pl
from jax.experimental.pallas import tpu as pltpu
from jax.sharding import PartitionSpec as P

DH = 128
SPAN = 64
LANES = 128
NEG = -1e30
FLOOR = -1e29
SCALE2 = math.log2(math.e) / math.sqrt(DH)
VMEM_BYTES = 48 * 1024 * 1024

PAIR = [(0, 1), (1, 0), (2, 3), (3, 2)]
MIDDLE = [(1, 2), (2, 1)]
INWARD = [(0, 1), (3, 2)]
OUTWARD = [(1, 0), (2, 3)]


def scores(query, key):
    return (
        lax.dot_general(query, key, (((1,), (1,)), ((), ())), preferred_element_type=jnp.float32)
        * SCALE2
    )


def self_kernel(flags, q_ref, k_ref, v_ref, *rest, group, blocks, rows):
    others, (out_ref, peak_ref, total_ref, accum_ref) = rest[:-4], rest[-4:]
    row = lax.broadcasted_iota(jnp.int32, (rows, rows), 0)
    col = lax.broadcasted_iota(jnp.int32, (rows, rows), 1)
    for g in range(group):
        cols = slice(g * DH, (g + 1) * DH)
        score = jnp.where(col <= row, scores(q_ref[:, cols], k_ref[:, cols]), NEG)
        peak = jnp.max(score, axis=-1, keepdims=True)
        weights = jnp.exp2(score - peak)
        total = jnp.sum(weights, axis=-1, keepdims=True)
        accum_ref[g] = jnp.dot(
            weights.astype(jnp.bfloat16), v_ref[:, cols], preferred_element_type=jnp.float32
        )
        peak_ref[g] = jnp.broadcast_to(peak, (rows, LANES))
        total_ref[g] = jnp.broadcast_to(total, (rows, LANES))
    for index, (operand, start) in enumerate(blocks):

        @pl.when(flags[index] == 1)
        def _(operand=operand, start=start):
            key_ref, value_ref = others[2 * operand], others[2 * operand + 1]
            for g in range(group):
                cols = slice(g * DH, (g + 1) * DH)
                score = scores(q_ref[:, cols], key_ref[start : start + rows, cols])
                before = peak_ref[g][:, :1]
                peak = jnp.maximum(before, jnp.max(score, axis=-1, keepdims=True))
                weights = jnp.exp2(score - peak)
                factor = jnp.exp2(before - peak)
                total = total_ref[g][:, :1] * factor + jnp.sum(weights, axis=-1, keepdims=True)
                accum_ref[g] = accum_ref[g] * factor + jnp.dot(
                    weights.astype(jnp.bfloat16),
                    value_ref[start : start + rows, cols],
                    preferred_element_type=jnp.float32,
                )
                peak_ref[g] = jnp.broadcast_to(peak, (rows, LANES))
                total_ref[g] = jnp.broadcast_to(total, (rows, LANES))

    for g in range(group):
        cols = slice(g * DH, (g + 1) * DH)
        out_ref[:, cols] = (accum_ref[g] / total_ref[g][:, :1]).astype(jnp.bfloat16)


def self_attention(flags, queries, keys, values, others, blocks):
    rows, width = queries.shape
    heads = width // DH
    group = math.gcd(heads, 4)

    def spec(array):
        return pl.BlockSpec((array.shape[0], group * DH), lambda h, flags: (0, h))

    operands = [queries, keys, values] + [array for pair in others for array in pair]
    pairs = (len(blocks) + 1) * rows * rows * heads
    return pl.pallas_call(
        functools.partial(self_kernel, group=group, blocks=blocks, rows=rows),
        out_shape=jax.ShapeDtypeStruct((rows, width), jnp.bfloat16),
        grid_spec=pltpu.PrefetchScalarGridSpec(
            num_scalar_prefetch=1,
            grid=(heads // group,),
            in_specs=[spec(array) for array in operands],
            out_specs=spec(queries),
            scratch_shapes=[
                pltpu.VMEM((group, rows, LANES), jnp.float32),
                pltpu.VMEM((group, rows, LANES), jnp.float32),
                pltpu.VMEM((group, rows, DH), jnp.float32),
            ],
        ),
        compiler_params=pltpu.CompilerParams(vmem_limit_bytes=VMEM_BYTES),
        cost_estimate=pl.CostEstimate(
            flops=4 * pairs * DH,
            bytes_accessed=sum(array.size * 2 for array in operands) + rows * width * 2,
            transcendentals=pairs,
        ),
        name="self_attention",
    )(flags, *operands)


def cross_kernel(meta, *refs, base, heads, group, span_count, near, two_queries, states, final):
    refs = list(refs)
    query_refs = [refs.pop(0) for _ in range(1 + two_queries)]
    database_ref = refs.pop(0)
    state_refs = [(refs.pop(0), refs.pop(0)) for _ in range(states)]
    out_ref = refs.pop(0)
    step = pl.program_id(0)
    width = heads * DH
    length = database_ref.shape[2]

    @pl.when(meta[base] == 1)
    def _():
        lane = lax.broadcasted_iota(jnp.int32, (SPAN, LANES), 1)
        for u in range(span_count):
            rows = slice(u * SPAN, (u + 1) * SPAN)
            places = [meta[base + 5 + u * near + n] for n in range(near)]
            stats = [
                jnp.where(meta[base + 3 + i] == 1, 1.0, 0.0) * ref[rows, :].astype(jnp.float32)
                for i, (_, ref) in enumerate(state_refs)
            ]
            coded = jnp.zeros((SPAN, LANES), jnp.float32)
            for g in range(group):
                cols = slice(g * DH, (g + 1) * DH)
                head = step * group + g
                mine = (lane == head) | (lane == heads + head) | (lane == 2 * heads + head)
                query = query_refs[0][rows, cols]
                if two_queries:
                    query = jnp.where(meta[base + 1] == 1, query, query_refs[1][rows, cols])
                found = []
                for place in places:
                    key = database_ref[0, jnp.maximum(place, 0), :, cols]
                    found.append(jnp.where(place >= 0, scores(query, key), NEG))
                came = []
                for i in range(states):
                    level = jnp.sum(jnp.where(mine, stats[i], 0.0), axis=-1, keepdims=True)
                    came.append(jnp.where(meta[base + 3 + i] == 1, level, NEG))
                peak = jnp.full((SPAN, 1), FLOOR, jnp.float32)
                for score in found:
                    peak = jnp.maximum(peak, jnp.max(score, axis=-1, keepdims=True))
                for level in came:
                    peak = jnp.maximum(peak, level)
                total = jnp.zeros((SPAN, 1), jnp.float32)
                accum = jnp.zeros((SPAN, DH), jnp.float32)
                for place, score in zip(places, found):
                    weights = jnp.exp2(score - peak)
                    total += jnp.sum(weights, axis=-1, keepdims=True)
                    accum += jnp.dot(
                        weights.astype(jnp.bfloat16),
                        database_ref[1, jnp.maximum(place, 0), :, cols],
                        preferred_element_type=jnp.float32,
                    )
                for i, level in enumerate(came):
                    factor = jnp.exp2(level - peak)
                    total += factor
                    accum += factor * jnp.where(
                        meta[base + 3 + i] == 1,
                        state_refs[i][0][rows, cols].astype(jnp.float32),
                        0.0,
                    )
                some = total > 0.0
                safe = jnp.where(some, total, 1.0)
                result = (accum / safe).astype(jnp.bfloat16)
                if final:
                    out_ref[rows, cols] = result
                    continue
                at = pl.multiple_of(step * (group * DH) + g * DH, DH)
                out_ref[rows, pl.ds(at, DH)] = result
                level = jnp.where(some, peak + jnp.log2(safe), NEG)
                high = level.astype(jnp.bfloat16).astype(jnp.float32)
                mid = (level - high).astype(jnp.bfloat16).astype(jnp.float32)
                low = level - high - mid
                coded += jnp.where(
                    lane == head,
                    high,
                    jnp.where(
                        lane == heads + head, mid, jnp.where(lane == 2 * heads + head, low, 0.0)
                    ),
                )
            if not final:
                before = jnp.where(step == 0, 0.0, 1.0) * jnp.where(
                    step == 0, 0.0, out_ref[rows, width:].astype(jnp.float32)
                )
                out_ref[rows, width:] = (before + coded).astype(jnp.bfloat16)


def cross_attention(meta, base, queries, database, states, final):
    rows, width = queries[0].shape
    heads = width // DH
    group = math.gcd(heads, 4)
    wide = group * DH
    near = (meta.shape[1] - 5) // (rows // SPAN)
    span_count = rows // SPAN
    at = base * meta.shape[1]
    per_owner, length = database.shape[1], database.shape[2]
    in_specs = [
        pl.BlockSpec((rows, wide), lambda h, meta, i=i: (0, h * meta[at + 1 + i]))
        for i in range(len(queries))
    ]
    in_specs.append(
        pl.BlockSpec(
            (2, per_owner, length, wide), lambda h, meta: (0, 0, 0, h * meta[at])
        )
    )
    operands = [*queries, database]
    for i, state in enumerate(states):
        in_specs.append(pl.BlockSpec((rows, wide), lambda h, meta, i=i: (0, h * meta[at + 3 + i])))
        in_specs.append(pl.BlockSpec((rows, LANES), lambda h, meta: (0, heads)))
        operands += [state, state]
    if final:
        out_width = width
        out_spec = pl.BlockSpec((rows, wide), lambda h, meta: (0, h))
    else:
        out_width = width + LANES
        out_spec = pl.BlockSpec((rows, out_width), lambda h, meta: (0, 0))
    pairs = rows * near * length * heads
    return pl.pallas_call(
        functools.partial(
            cross_kernel,
            base=at,
            heads=heads,
            group=group,
            span_count=span_count,
            near=near,
            two_queries=len(queries) - 1,
            states=len(states),
            final=final,
        ),
        out_shape=jax.ShapeDtypeStruct((rows, out_width), jnp.bfloat16),
        grid_spec=pltpu.PrefetchScalarGridSpec(
            num_scalar_prefetch=1,
            grid=(heads // group,),
            in_specs=in_specs,
            out_specs=out_spec,
        ),
        compiler_params=pltpu.CompilerParams(vmem_limit_bytes=VMEM_BYTES),
        cost_estimate=pl.CostEstimate(
            flops=4 * pairs * DH,
            bytes_accessed=database.size * 2 + rows * width * 2 * (2 + len(states)),
            transcendentals=pairs,
        ),
        name="cross_attention",
    )(meta.reshape(-1), *operands)


def project_kernel(meta, x_ref, *refs, sides, depth, columns, tile):
    count = 1 + sum(len(side) for side in sides)
    weight_refs, (out_ref, held, sems) = refs[:count], refs[count:]
    own = [(weight_refs[0], 0, depth)]
    lists = []
    taken = 1
    for side in sides:
        lists.append(
            [
                (ref, offset if isinstance(offset, int) else meta[offset[0]], size)
                for ref, (offset, size) in zip(weight_refs[taken : taken + len(side)], side)
            ]
        )
        taken += len(side)

    def run(first, second):
        copies = []
        for slot, pieces in enumerate((first, second)):
            copies.append([])
            for index, (ref, offset, size) in enumerate(pieces):
                if not isinstance(offset, int):
                    offset = pl.multiple_of(offset, size)
                copy = pltpu.make_async_copy(
                    ref, held.at[slot, pl.ds(offset, size), :], sems.at[slot, index]
                )
                copy.start()
                copies[-1].append(copy)
        for slot in range(2):
            for copy in copies[slot]:
                copy.wait()

            @pl.loop(0, columns // tile)
            def _(n, slot=slot):
                part = pl.multiple_of(n * tile, tile)
                place = pl.multiple_of(meta[2 + slot] * columns + n * tile, tile)
                out_ref[:, pl.ds(place, tile)] = jnp.dot(
                    x_ref[...],
                    held[slot, :, pl.ds(part, tile)],
                    preferred_element_type=jnp.float32,
                ).astype(jnp.bfloat16)

    @pl.when((meta[0] == 1) & (meta[1] == 0))
    def _():
        run(own, lists[0])

    @pl.when((meta[0] == 1) & (meta[1] == 1))
    def _():
        run(lists[1], lists[2])


def project(meta, x, weight, sides):
    rows, depth = x.shape
    columns = weight.shape[1]
    operands = [weight] + [array for side in sides for array, _ in side]
    most = max(len(side) for side in sides)
    shapes = [[(offset, array.shape[0]) for array, offset in side] for side in sides]
    return pl.pallas_call(
        functools.partial(
            project_kernel, sides=shapes, depth=depth, columns=columns, tile=min(256, columns)
        ),
        out_shape=jax.ShapeDtypeStruct((rows, 2 * columns), jnp.bfloat16),
        in_specs=[pl.BlockSpec(memory_space=pltpu.SMEM), pl.BlockSpec(memory_space=pltpu.VMEM)]
        + [pl.BlockSpec(memory_space=pl.ANY)] * len(operands),
        out_specs=pl.BlockSpec(memory_space=pltpu.VMEM),
        scratch_shapes=[
            pltpu.VMEM((2, depth, columns), jnp.bfloat16),
            pltpu.SemaphoreType.DMA((2, most)),
        ],
        compiler_params=pltpu.CompilerParams(vmem_limit_bytes=VMEM_BYTES),
        cost_estimate=pl.CostEstimate(
            flops=4 * rows * depth * columns,
            bytes_accessed=4 * depth * columns + 2 * rows * (depth + 2 * columns),
            transcendentals=0,
        ),
        name="project",
    )(meta, x, *operands)


def after(value, *earlier):
    return lax.optimization_barrier((value, *earlier))[0]


def shards(hidden_in, queries, keys, values, cross_queries, neighbours, database, out_weight):
    rows, width = queries.shape[1:]
    member_count = lax.axis_size("ctx")
    part_count = lax.axis_size("tp")
    assert lax.axis_size("db") == 4
    member = lax.axis_index("ctx")
    plane = lax.axis_index("db")
    part = lax.axis_index("tp")
    outer = (plane == 0) | (plane == 3)
    inner = jnp.logical_not(outer)
    two_level = member_count == 4
    CORE = [(0, 1), (1, 0), (2, 3), (3, 2)]
    ACROSS = [(0, 2), (1, 3), (2, 0), (3, 1)]

    def send(value, perm, axis="db"):
        return lax.ppermute(value, axis, perm)

    query = cross_queries[0]
    ids = lax.all_gather(neighbours[0].reshape(-1), "db")
    query_a = send(query, PAIR)
    query_m = send(query, MIDDLE)

    key, value = keys[0], values[0]
    if two_level:
        key_y = send(key, [(0, 2), (1, 3)], "ctx")
        value_y = send(value, [(0, 2), (1, 3)], "ctx")
        key_c = send(key, [(0, 1), (2, 3)], "ctx")
        value_c = send(value, [(0, 1), (2, 3)], "ctx")
        key_yc = send(key_y, [(2, 3), (3, 2)], "ctx")
        value_yc = send(value_y, [(2, 3), (3, 2)], "ctx")
        flags = jnp.stack([member % 2, member // 2, member // 2]).astype(jnp.int32)
        others = [(key_c, value_c), (key_y, value_y), (key_yc, value_yc)]
        blocks = [(0, 0), (1, 0), (2, 0)]
    else:
        others = [
            (
                lax.all_gather(key, "ctx", axis=0, tiled=True),
                lax.all_gather(value, "ctx", axis=0, tiled=True),
            )
        ]
        blocks = [(0, j * rows) for j in range(member_count)]
        flags = (jnp.arange(member_count) < member).astype(jnp.int32)

    depth = out_weight.shape[0]
    share = depth // member_count
    own_share = lax.dynamic_slice_in_dim(out_weight, member * share, share, axis=0)
    query_c = send(query_a, MIDDLE)
    query_b_out = send(query_m, OUTWARD)
    share_a = send(after(own_share, query_a), INWARD)
    share_b = send(after(own_share, query_c), MIDDLE)
    share_c = send(after(share_a, share_b), MIDDLE)
    query_c_out = send(after(query_c, query_b_out), OUTWARD)

    def whole(piece):
        if not two_level:
            return [(lax.all_gather(piece, "ctx", axis=0, tiled=True), 0)]
        across = send(piece, ACROSS, "ctx")
        beside = send(piece, CORE, "ctx")
        corner = send(across, CORE, "ctx")
        return [(piece, (4,)), (across, (5,)), (beside, (6,)), (corner, (7,))]

    per_owner = database.shape[1]
    local = jnp.where(ids // per_owner == plane, ids % per_owner, -1)
    seq_a = plane ^ 1
    seq_b = jnp.where(plane < 2, 2, 1)
    seq_c = jnp.where(plane < 2, 3, 0)
    one = jnp.ones((), jnp.int32)
    zero = jnp.zeros((), jnp.int32)
    is_outer = outer.astype(jnp.int32)
    is_inner = inner.astype(jnp.int32)

    def described(active, first, second, state, other, seq):
        head = jnp.stack([active, first, second, state, other]).astype(jnp.int32)
        return jnp.concatenate([head, lax.dynamic_index_in_dim(local, seq, 0, keepdims=False)])

    meta = jnp.stack(
        [
            described(is_outer, is_outer, zero, zero, zero, plane),
            described(is_outer, is_outer, zero, zero, zero, seq_c),
            described(one, is_outer, is_inner, is_inner, zero, jnp.where(outer, seq_b, seq_c)),
            described(one, is_outer, is_inner, is_inner, zero, jnp.where(outer, seq_a, seq_b)),
            described(is_inner, is_inner, zero, is_inner, is_inner, seq_a),
            described(is_inner, is_inner, zero, is_inner, is_inner, plane),
        ]
    )

    def cross(call, call_queries, states=(), final=False):
        return cross_attention(meta, call, call_queries, database, states, final)

    own_part = send(after(cross(0, [query]), share_a), INWARD)
    in_1 = send(cross(1, [query_c_out]), INWARD)
    pieces_a, pieces_b, pieces_c = whole(share_a), whole(share_b), whole(share_c)
    part_2 = cross(2, [query_b_out, query_c], [in_1])
    in_2 = send(part_2, INWARD)
    mid_2 = send(part_2, MIDDLE)
    part_3 = cross(3, [query_a, query_m], [in_2])
    in_3 = send(part_3, INWARD)
    mid_3 = send(part_3, MIDDLE)
    cross_a = cross(4, [query_a], [mid_2, own_part], final=True)

    side = plane // 2
    offsets = [member * share, (member ^ 2) * share, (member ^ 1) * share, (member ^ 3) * share]

    def projected(x, half):
        group = jnp.where(side == half, 0, 1)
        first = jnp.where(group == 0, plane % 2, seq_b % 2)
        second = jnp.where(group == 0, seq_a % 2, seq_c % 2)
        numbers = jnp.stack([is_inner, group, first, second, *offsets]).astype(jnp.int32)
        return project(numbers, x, out_weight, [pieces_a, pieces_b, pieces_c])

    def reduced(x):
        if part_count != 2:
            both = jnp.concatenate([projected(x, 0), projected(x, 1)], axis=1)
            return lax.psum_scatter(both, "tp", scatter_dimension=1, tiled=True).astype(
                jnp.float32
            )
        got = send(projected(x, 1 - part), [(0, 1), (1, 0)], "tp")
        kept = projected(x, part)
        return kept.astype(jnp.float32) + got.astype(jnp.float32)

    for_outer = send(reduced(cross_a).astype(jnp.bfloat16), OUTWARD)
    cross_own = cross(5, [query], [in_3, mid_3], final=True)
    summed = jnp.where(outer, for_outer.astype(jnp.float32), reduced(cross_own))
    mixed = (hidden_in[0].astype(jnp.float32) + summed).astype(jnp.bfloat16)

    attended = self_attention(flags, queries[0], key, value, others, blocks)
    return (attended[None], mixed[None])


def solution(mesh):
    in_specs = (
        P("db", "ctx", "tp"),
        P("db", "ctx", "tp"),
        P("db", "ctx", "tp"),
        P("db", "ctx", "tp"),
        P("db", "ctx", "tp"),
        P("db", "ctx", None),
        P(None, "db", None, "tp"),
        P("tp", "db"),
    )
    out_specs = (P("db", "ctx", "tp"), P("db", "ctx", "tp"))
    return jax.shard_map(shards, mesh=mesh, in_specs=in_specs, out_specs=out_specs, check_vma=False)
```

```python
import functools
import math

import jax
import jax.numpy as jnp
from jax import lax
from jax.experimental import pallas as pl
from jax.experimental.pallas import tpu as pltpu
from jax.sharding import PartitionSpec as P

DH = 128
SPAN = 64
LANES = 128
NEG = -1e30
FLOOR = -1e29
SCALE2 = math.log2(math.e) / math.sqrt(DH)
VMEM_BYTES = 48 * 1024 * 1024

PAIR = [(0, 1), (1, 0), (2, 3), (3, 2)]
MIDDLE = [(1, 2), (2, 1)]
INWARD = [(0, 1), (3, 2)]
OUTWARD = [(1, 0), (2, 3)]


def scores(query, key):
    return (
        lax.dot_general(query, key, (((1,), (1,)), ((), ())), preferred_element_type=jnp.float32)
        * SCALE2
    )


def with_ones(value):
    return jnp.concatenate([value, jnp.ones_like(value)], axis=1)


def case_kernel(chosen_ref, q_ref, k_ref, v_ref, *rest, group, cases, rows):
    others, out_ref = rest[:-1], rest[-1]
    some = [slice(g * DH, (g + 1) * DH) for g in range(group)]

    def run(chosen):
        row = lax.broadcasted_iota(jnp.int32, (rows, rows), 0)
        col = lax.broadcasted_iota(jnp.int32, (rows, rows), 1)
        pairs = [(k_ref, v_ref)] + [(others[2 * i], others[2 * i + 1]) for i in chosen]
        found = [[scores(q_ref[:, c], key[:, c]) for key, _ in pairs] for c in some]
        for score in found:
            score[0] = jnp.where(col <= row, score[0], NEG)
        peaks = [
            jnp.max(functools.reduce(jnp.maximum, score), axis=-1, keepdims=True) for score in found
        ]
        weights = [
            [jnp.exp2(part - peak).astype(jnp.bfloat16) for part in score]
            for score, peak in zip(found, peaks)
        ]
        for c, parts in zip(some, weights):
            both = sum(
                jnp.dot(part, with_ones(value[:, c]), preferred_element_type=jnp.float32)
                for part, (_, value) in zip(parts, pairs)
            )
            out_ref[:, c] = (both[:, :DH] / both[:, DH:]).astype(jnp.bfloat16)

    for index, chosen in enumerate(cases):
        pl.when(chosen_ref[0] == index)(functools.partial(run, chosen))


def self_attention_cases(chosen, queries, keys, values, others, cases):
    rows, width = queries.shape
    heads = width // DH
    group = math.gcd(heads, 4)
    spec = pl.BlockSpec((rows, group * DH), lambda h, chosen: (0, h))
    operands = [queries, keys, values] + [array for pair in others for array in pair]
    pairs = (len(others) + 1) * rows * rows * heads
    return pl.pallas_call(
        functools.partial(case_kernel, group=group, cases=cases, rows=rows),
        out_shape=jax.ShapeDtypeStruct((rows, width), jnp.bfloat16),
        grid_spec=pltpu.PrefetchScalarGridSpec(
            num_scalar_prefetch=1,
            grid=(heads // group,),
            in_specs=[spec] * len(operands),
            out_specs=spec,
        ),
        compiler_params=pltpu.CompilerParams(vmem_limit_bytes=VMEM_BYTES),
        cost_estimate=pl.CostEstimate(
            flops=4 * pairs * DH,
            bytes_accessed=(len(operands) + 1) * rows * width * 2,
            transcendentals=pairs,
        ),
        name="self_attention",
    )(chosen, *operands)


def self_kernel(flags, q_ref, k_ref, v_ref, *rest, group, blocks, rows):
    others, (out_ref, peak_ref, total_ref, accum_ref) = rest[:-4], rest[-4:]
    row = lax.broadcasted_iota(jnp.int32, (rows, rows), 0)
    col = lax.broadcasted_iota(jnp.int32, (rows, rows), 1)
    for g in range(group):
        cols = slice(g * DH, (g + 1) * DH)
        score = jnp.where(col <= row, scores(q_ref[:, cols], k_ref[:, cols]), NEG)
        peak = jnp.max(score, axis=-1, keepdims=True)
        weights = jnp.exp2(score - peak)
        total = jnp.sum(weights, axis=-1, keepdims=True)
        accum_ref[g] = jnp.dot(
            weights.astype(jnp.bfloat16), v_ref[:, cols], preferred_element_type=jnp.float32
        )
        peak_ref[g] = jnp.broadcast_to(peak, (rows, LANES))
        total_ref[g] = jnp.broadcast_to(total, (rows, LANES))
    for index, (operand, start) in enumerate(blocks):

        @pl.when(flags[index] == 1)
        def _(operand=operand, start=start):
            key_ref, value_ref = others[2 * operand], others[2 * operand + 1]
            for g in range(group):
                cols = slice(g * DH, (g + 1) * DH)
                score = scores(q_ref[:, cols], key_ref[start : start + rows, cols])
                before = peak_ref[g][:, :1]
                peak = jnp.maximum(before, jnp.max(score, axis=-1, keepdims=True))
                weights = jnp.exp2(score - peak)
                factor = jnp.exp2(before - peak)
                total = total_ref[g][:, :1] * factor + jnp.sum(weights, axis=-1, keepdims=True)
                accum_ref[g] = accum_ref[g] * factor + jnp.dot(
                    weights.astype(jnp.bfloat16),
                    value_ref[start : start + rows, cols],
                    preferred_element_type=jnp.float32,
                )
                peak_ref[g] = jnp.broadcast_to(peak, (rows, LANES))
                total_ref[g] = jnp.broadcast_to(total, (rows, LANES))

    for g in range(group):
        cols = slice(g * DH, (g + 1) * DH)
        out_ref[:, cols] = (accum_ref[g] / total_ref[g][:, :1]).astype(jnp.bfloat16)


def self_attention(flags, queries, keys, values, others, blocks):
    rows, width = queries.shape
    heads = width // DH
    group = math.gcd(heads, 4)

    def spec(array):
        return pl.BlockSpec((array.shape[0], group * DH), lambda h, flags: (0, h))

    operands = [queries, keys, values] + [array for pair in others for array in pair]
    pairs = (len(blocks) + 1) * rows * rows * heads
    return pl.pallas_call(
        functools.partial(self_kernel, group=group, blocks=blocks, rows=rows),
        out_shape=jax.ShapeDtypeStruct((rows, width), jnp.bfloat16),
        grid_spec=pltpu.PrefetchScalarGridSpec(
            num_scalar_prefetch=1,
            grid=(heads // group,),
            in_specs=[spec(array) for array in operands],
            out_specs=spec(queries),
            scratch_shapes=[
                pltpu.VMEM((group, rows, LANES), jnp.float32),
                pltpu.VMEM((group, rows, LANES), jnp.float32),
                pltpu.VMEM((group, rows, DH), jnp.float32),
            ],
        ),
        compiler_params=pltpu.CompilerParams(vmem_limit_bytes=VMEM_BYTES),
        cost_estimate=pl.CostEstimate(
            flops=4 * pairs * DH,
            bytes_accessed=sum(array.size * 2 for array in operands) + rows * width * 2,
            transcendentals=pairs,
        ),
        name="self_attention",
    )(flags, *operands)


def cross_kernel(meta, *refs, base, heads, group, span_count, near, two_queries, states, final):
    refs = list(refs)
    query_refs = [refs.pop(0) for _ in range(1 + two_queries)]
    database_ref = refs.pop(0)
    state_refs = [refs.pop(0) for _ in range(states)]
    out_ref, query, came, held, peak_ref, total_ref, accum_ref, sems, more = refs
    width = heads * DH
    rows = span_count * SPAN
    entries = span_count * near
    used = [meta[base + 3 + i] == 1 for i in range(states)]
    every = [slice(h * DH, (h + 1) * DH) for h in range(heads)]

    def fetch(entry, index):
        place = jnp.maximum(meta[base + 5 + entry], 0)
        return pltpu.make_async_copy(
            database_ref.at[index, place], held.at[index, entry], sems.at[index, entry]
        )

    @pl.when(meta[base] == 1)
    def _():
        gets = [
            pltpu.make_async_copy(ref, came.at[i], more.at[1 + i])
            for i, ref in enumerate(state_refs)
        ]
        for i, get in enumerate(gets):
            pl.when(used[i])(get.start)
        picks = [pltpu.make_async_copy(ref, query, more.at[0]) for ref in query_refs]
        if two_queries:
            pl.when(meta[base + 1] == 1)(picks[0].start)
            pl.when(meta[base + 1] == 0)(picks[1].start)
        else:
            picks[0].start()
        for entry in range(entries):

            @pl.when(meta[base + 5 + entry] >= 0)
            def _(entry=entry):
                fetch(entry, 0).start()
                fetch(entry, 1).start()

        lane = lax.broadcasted_iota(jnp.int32, (1, LANES), 1)
        line = lax.broadcasted_iota(jnp.int32, (LANES, LANES), 0)
        for i, get in enumerate(gets):
            pl.when(used[i])(get.wait)
        if states:
            stats = [came[i, :, width:] for i in range(states)]
            for h, cols in enumerate(every):
                spread = (line == h) | (line == heads + h) | (line == 2 * heads + h)
                levels = [
                    jnp.where(
                        used[i],
                        jnp.dot(
                            stats[i],
                            spread.astype(jnp.bfloat16),
                            preferred_element_type=jnp.float32,
                        ),
                        NEG,
                    )
                    for i in range(states)
                ]
                peak = jnp.full((rows, LANES), FLOOR, jnp.float32)
                for level in levels:
                    peak = jnp.maximum(peak, level)
                factors = [jnp.exp2(level - peak) for level in levels]
                peak_ref[:, cols] = peak
                total_ref[:, cols] = sum(factors)
                accum_ref[:, cols] = sum(
                    jnp.where(used[i], factor * came[i, :, cols].astype(jnp.float32), 0.0)
                    for i, factor in enumerate(factors)
                )
        else:
            peak_ref[...] = jnp.full((rows, width), FLOOR, jnp.float32)
            total_ref[...] = jnp.zeros((rows, width), jnp.float32)
            accum_ref[...] = jnp.zeros((rows, width), jnp.float32)
        picks[0].wait()

        @pl.loop(0, entries)
        def _(entry):
            @pl.when(meta[base + 5 + entry] >= 0)
            def _():
                fetch(entry, 0).wait()
                fetch(entry, 1).wait()
                here = pl.ds(pl.multiple_of((entry // near) * SPAN, SPAN), SPAN)
                for start in range(0, heads, group):
                    some = every[start : start + group]
                    found = [scores(query[here, c], held[0, entry, :, c]) for c in some]
                    before = [peak_ref[here, c] for c in some]
                    peaks = [
                        jnp.maximum(old, jnp.max(score, axis=-1, keepdims=True))
                        for old, score in zip(before, found)
                    ]
                    weights = [
                        jnp.exp2(score - peak).astype(jnp.bfloat16)
                        for score, peak in zip(found, peaks)
                    ]
                    factors = [jnp.exp2(old - peak) for old, peak in zip(before, peaks)]
                    both = [
                        jnp.dot(
                            weight,
                            with_ones(held[1, entry, :, c]),
                            preferred_element_type=jnp.float32,
                        )
                        for weight, c in zip(weights, some)
                    ]
                    accums = [
                        accum_ref[here, c] * factor + pair[:, :DH]
                        for c, factor, pair in zip(some, factors, both)
                    ]
                    totals = [
                        total_ref[here, c] * factor + pair[:, DH:]
                        for c, factor, pair in zip(some, factors, both)
                    ]
                    for c, peak, accum, total in zip(some, peaks, accums, totals):
                        peak_ref[here, c] = peak
                        accum_ref[here, c] = accum
                        total_ref[here, c] = total

        packed = jnp.zeros((rows, LANES), jnp.float32)
        for h, cols in enumerate(every):
            total = total_ref[:, cols]
            safe = jnp.where(total > 0.0, total, 1.0)
            out_ref[:, cols] = (accum_ref[:, cols] / safe).astype(jnp.bfloat16)
            if not final:
                level = jnp.where(total > 0.0, peak_ref[:, cols] + jnp.log2(safe), NEG)
                packed = jnp.where(lane == h, level, packed)
        if not final:
            high = packed.astype(jnp.bfloat16).astype(jnp.float32)
            mid = (packed - high).astype(jnp.bfloat16).astype(jnp.float32)
            low = packed - high - mid
            coded = high + pltpu.roll(mid, heads, 1) + pltpu.roll(low, 2 * heads, 1)
            out_ref[:, width:] = coded.astype(jnp.bfloat16)


def cross_attention(meta, base, queries, database, states, final):
    rows, width = queries[0].shape
    heads = width // DH
    assert 3 * heads <= LANES
    span_count = rows // SPAN
    near = (meta.shape[1] - 5) // span_count
    entries = span_count * near
    length = database.shape[2]
    out_width = width if final else width + LANES
    anywhere = pl.BlockSpec(memory_space=pl.ANY)
    pairs = rows * near * length * heads // 4
    return pl.pallas_call(
        functools.partial(
            cross_kernel,
            base=base * meta.shape[1],
            heads=heads,
            group=heads,
            span_count=span_count,
            near=near,
            two_queries=len(queries) - 1,
            states=len(states),
            final=final,
        ),
        out_shape=jax.ShapeDtypeStruct((rows, out_width), jnp.bfloat16),
        in_specs=[pl.BlockSpec(memory_space=pltpu.SMEM)]
        + [anywhere] * (len(queries) + 1 + len(states)),
        out_specs=pl.BlockSpec(memory_space=pltpu.VMEM),
        scratch_shapes=[
            pltpu.VMEM((rows, width), jnp.bfloat16),
            pltpu.VMEM((max(len(states), 1), rows, width + LANES), jnp.bfloat16),
            pltpu.VMEM((2, entries, length, width), jnp.bfloat16),
            pltpu.VMEM((rows, width), jnp.float32),
            pltpu.VMEM((rows, width), jnp.float32),
            pltpu.VMEM((rows, width), jnp.float32),
            pltpu.SemaphoreType.DMA((2, entries)),
            pltpu.SemaphoreType.DMA((3,)),
        ],
        compiler_params=pltpu.CompilerParams(vmem_limit_bytes=VMEM_BYTES),
        cost_estimate=pl.CostEstimate(
            flops=4 * pairs * DH,
            bytes_accessed=database.size // 2 + rows * width * 2 * (2 + len(states)),
            transcendentals=pairs,
        ),
        name="cross_attention",
    )(meta.reshape(-1), *queries, database, *states)


def project_kernel(meta, x_ref, *refs, sides, depth, columns, tile):
    count = 1 + sum(len(side) for side in sides)
    weight_refs, (out_ref, held, sems) = refs[:count], refs[count:]
    own = [(weight_refs[0], 0, depth)]
    lists = []
    taken = 1
    for side in sides:
        lists.append(
            [
                (ref, offset if isinstance(offset, int) else meta[offset[0]], size)
                for ref, (offset, size) in zip(weight_refs[taken : taken + len(side)], side)
            ]
        )
        taken += len(side)

    def run(first, second):
        copies = []
        for slot, pieces in enumerate((first, second)):
            copies.append([])
            for index, (ref, offset, size) in enumerate(pieces):
                if not isinstance(offset, int):
                    offset = pl.multiple_of(offset, size)
                copy = pltpu.make_async_copy(
                    ref, held.at[slot, pl.ds(offset, size), :], sems.at[slot, index]
                )
                copy.start()
                copies[-1].append(copy)
        for slot in range(2):
            for copy in copies[slot]:
                copy.wait()

            @pl.loop(0, columns // tile)
            def _(n, slot=slot):
                part = pl.multiple_of(n * tile, tile)
                place = pl.multiple_of(meta[2 + slot] * columns + n * tile, tile)
                out_ref[:, pl.ds(place, tile)] = jnp.dot(
                    x_ref[...],
                    held[slot, :, pl.ds(part, tile)],
                    preferred_element_type=jnp.float32,
                ).astype(jnp.bfloat16)

    @pl.when((meta[0] == 1) & (meta[1] == 0))
    def _():
        run(own, lists[0])

    @pl.when((meta[0] == 1) & (meta[1] == 1))
    def _():
        run(lists[1], lists[2])


def project(meta, x, weight, sides):
    rows, depth = x.shape
    columns = weight.shape[1]
    operands = [weight] + [array for side in sides for array, _ in side]
    most = max(len(side) for side in sides)
    shapes = [[(offset, array.shape[0]) for array, offset in side] for side in sides]
    return pl.pallas_call(
        functools.partial(
            project_kernel, sides=shapes, depth=depth, columns=columns, tile=min(256, columns)
        ),
        out_shape=jax.ShapeDtypeStruct((rows, 2 * columns), jnp.bfloat16),
        in_specs=[pl.BlockSpec(memory_space=pltpu.SMEM), pl.BlockSpec(memory_space=pltpu.VMEM)]
        + [pl.BlockSpec(memory_space=pl.ANY)] * len(operands),
        out_specs=pl.BlockSpec(memory_space=pltpu.VMEM),
        scratch_shapes=[
            pltpu.VMEM((2, depth, columns), jnp.bfloat16),
            pltpu.SemaphoreType.DMA((2, most)),
        ],
        compiler_params=pltpu.CompilerParams(vmem_limit_bytes=VMEM_BYTES),
        cost_estimate=pl.CostEstimate(
            flops=4 * rows * depth * columns,
            bytes_accessed=4 * depth * columns + 2 * rows * (depth + 2 * columns),
            transcendentals=0,
        ),
        name="project",
    )(meta, x, *operands)


def after(value, *earlier):
    return lax.optimization_barrier((value, *earlier))[0]


def shards(hidden_in, queries, keys, values, cross_queries, neighbours, database, out_weight):
    rows, width = queries.shape[1:]
    member_count = lax.axis_size("ctx")
    part_count = lax.axis_size("tp")
    assert lax.axis_size("db") == 4
    member = lax.axis_index("ctx")
    plane = lax.axis_index("db")
    part = lax.axis_index("tp")
    outer = (plane == 0) | (plane == 3)
    inner = jnp.logical_not(outer)
    two_level = member_count == 4
    CORE = [(0, 1), (1, 0), (2, 3), (3, 2)]
    ACROSS = [(0, 2), (1, 3), (2, 0), (3, 1)]

    def send(value, perm, axis="db"):
        return lax.ppermute(value, axis, perm)

    query = cross_queries[0]
    query_a = send(query, PAIR)
    query_m = send(query, MIDDLE)
    own_ids = neighbours[0].reshape(-1)
    ids = [own_ids] + [
        send(own_ids, [(i, (i + step) % 4) for i in range(4)]) for step in range(1, 4)
    ]

    key, value = keys[0], values[0]
    if two_level:
        key_y = send(key, [(0, 2), (1, 3)], "ctx")
        value_y = send(value, [(0, 2), (1, 3)], "ctx")
        key_c = send(key, [(0, 1), (2, 3)], "ctx")
        value_c = send(value, [(0, 1), (2, 3)], "ctx")
        key_yc = send(key_y, [(2, 3), (3, 2)], "ctx")
        value_yc = send(value_y, [(2, 3), (3, 2)], "ctx")
        attended = self_attention_cases(
            member.astype(jnp.int32)[None],
            queries[0],
            key,
            value,
            [(key_c, value_c), (key_y, value_y), (key_yc, value_yc)],
            [[], [0], [1, 2], [0, 1, 2]],
        )
    else:
        others = [
            (
                lax.all_gather(key, "ctx", axis=0, tiled=True),
                lax.all_gather(value, "ctx", axis=0, tiled=True),
            )
        ]
        blocks = [(0, j * rows) for j in range(member_count)]
        flags = (jnp.arange(member_count) < member).astype(jnp.int32)
        attended = self_attention(flags, queries[0], key, value, others, blocks)

    depth = out_weight.shape[0]
    share = depth // member_count
    own_share = lax.dynamic_slice_in_dim(out_weight, member * share, share, axis=0)
    query_c = send(query_a, MIDDLE)
    query_b_out = send(query_m, OUTWARD)
    share_a = send(after(own_share, query_a), INWARD)
    share_b = send(after(own_share, query_c), MIDDLE)
    share_c = send(after(share_a, share_b), MIDDLE)
    waited = (key_y, value_y) if two_level else ()
    query_c_out = send(after(query_c, query_b_out, *waited), OUTWARD)

    def whole(piece):
        if not two_level:
            return [(lax.all_gather(piece, "ctx", axis=0, tiled=True), 0)]
        across = send(piece, ACROSS, "ctx")
        beside = send(piece, CORE, "ctx")
        corner = send(across, CORE, "ctx")
        return [(piece, (4,)), (across, (5,)), (beside, (6,)), (corner, (7,))]

    per_owner = database.shape[1]
    ids = jnp.stack(ids)
    local = jnp.where(ids // per_owner == plane, ids % per_owner, -1)
    seq_a = plane ^ 1
    seq_b = jnp.where(plane < 2, 2, 1)
    seq_c = jnp.where(plane < 2, 3, 0)
    one = jnp.ones((), jnp.int32)
    zero = jnp.zeros((), jnp.int32)
    is_outer = outer.astype(jnp.int32)
    is_inner = inner.astype(jnp.int32)

    def described(active, first, second, state, other, seq):
        head = jnp.stack([active, first, second, state, other]).astype(jnp.int32)
        return jnp.concatenate([head, lax.dynamic_index_in_dim(local, (plane - seq) % 4, 0, keepdims=False)])

    meta = jnp.stack(
        [
            described(is_outer, is_outer, zero, zero, zero, plane),
            described(is_outer, is_outer, zero, zero, zero, seq_c),
            described(one, is_outer, is_inner, is_inner, zero, jnp.where(outer, seq_b, seq_c)),
            described(one, is_outer, is_inner, is_inner, zero, jnp.where(outer, seq_a, seq_b)),
            described(is_inner, is_inner, zero, is_inner, is_inner, seq_a),
            described(is_inner, is_inner, zero, is_inner, is_inner, plane),
        ]
    )

    def cross(call, call_queries, states=(), final=False):
        return cross_attention(meta, call, call_queries, database, states, final)

    own_part = send(after(cross(0, [query]), share_a), INWARD)
    in_1 = send(cross(1, [query_c_out]), INWARD)
    pieces_a, pieces_b, pieces_c = whole(share_a), whole(share_b), whole(share_c)
    part_2 = cross(2, [query_b_out, after(query_c, attended)], [in_1])
    in_2 = send(part_2, INWARD)
    mid_2 = send(part_2, MIDDLE)
    part_3 = cross(3, [query_a, query_m], [in_2])
    in_3 = send(part_3, INWARD)
    mid_3 = send(part_3, MIDDLE)
    cross_a = cross(4, [query_a], [mid_2, own_part], final=True)

    side = plane // 2
    offsets = [member * share, (member ^ 2) * share, (member ^ 1) * share, (member ^ 3) * share]

    def projected(x, half):
        group = jnp.where(side == half, 0, 1)
        first = jnp.where(group == 0, plane % 2, seq_b % 2)
        second = jnp.where(group == 0, seq_a % 2, seq_c % 2)
        numbers = jnp.stack([is_inner, group, first, second, *offsets]).astype(jnp.int32)
        return project(numbers, x, out_weight, [pieces_a, pieces_b, pieces_c])

    def reduced(x):
        if part_count != 2:
            both = jnp.concatenate([projected(x, 0), projected(x, 1)], axis=1)
            return lax.psum_scatter(both, "tp", scatter_dimension=1, tiled=True).astype(
                jnp.float32
            )
        got = send(projected(x, 1 - part), [(0, 1), (1, 0)], "tp")
        kept = projected(x, part)
        return kept.astype(jnp.float32) + got.astype(jnp.float32)

    for_outer = send(reduced(cross_a).astype(jnp.bfloat16), OUTWARD)
    cross_own = cross(5, [query], [in_3, mid_3], final=True)
    summed = jnp.where(outer, for_outer.astype(jnp.float32), reduced(cross_own))
    mixed = (hidden_in[0].astype(jnp.float32) + summed).astype(jnp.bfloat16)

    return (attended[None], mixed[None])


def solution(mesh):
    in_specs = (
        P("db", "ctx", "tp"),
        P("db", "ctx", "tp"),
        P("db", "ctx", "tp"),
        P("db", "ctx", "tp"),
        P("db", "ctx", "tp"),
        P("db", "ctx", None),
        P(None, "db", None, "tp"),
        P("tp", "db"),
    )
    out_specs = (P("db", "ctx", "tp"), P("db", "ctx", "tp"))
    return jax.shard_map(shards, mesh=mesh, in_specs=in_specs, out_specs=out_specs, check_vma=False)
```

```python
import functools
import math

import jax
import jax.numpy as jnp
from jax import lax
from jax.experimental import pallas as pl
from jax.experimental.pallas import tpu as pltpu
from jax.sharding import PartitionSpec as P

DH = 128
PARTS = 1
SPAN = 64
LANES = 128
NEG = -1e30
FLOOR = -1e29
SCALE2 = math.log2(math.e) / math.sqrt(DH)
VMEM_BYTES = 48 * 1024 * 1024

PAIR = [(0, 1), (1, 0), (2, 3), (3, 2)]
MIDDLE = [(1, 2), (2, 1)]
INWARD = [(0, 1), (3, 2)]
OUTWARD = [(1, 0), (2, 3)]


def scores(query, key):
    return (
        lax.dot_general(query, key, (((1,), (1,)), ((), ())), preferred_element_type=jnp.float32)
        * SCALE2
    )


def with_ones(value):
    return jnp.concatenate([value, jnp.ones_like(value)], axis=1)


def self_kernel(flags, q_ref, k_ref, v_ref, *rest, group, blocks, rows):
    others, (out_ref, peak_ref, total_ref, accum_ref) = rest[:-4], rest[-4:]
    row = lax.broadcasted_iota(jnp.int32, (rows, rows), 0)
    col = lax.broadcasted_iota(jnp.int32, (rows, rows), 1)
    for g in range(group):
        cols = slice(g * DH, (g + 1) * DH)
        score = jnp.where(col <= row, scores(q_ref[:, cols], k_ref[:, cols]), NEG)
        peak = jnp.max(score, axis=-1, keepdims=True)
        weights = jnp.exp2(score - peak)
        total = jnp.sum(weights, axis=-1, keepdims=True)
        accum_ref[g] = jnp.dot(
            weights.astype(jnp.bfloat16), v_ref[:, cols], preferred_element_type=jnp.float32
        )
        peak_ref[g] = jnp.broadcast_to(peak, (rows, LANES))
        total_ref[g] = jnp.broadcast_to(total, (rows, LANES))
    for index, (operand, start) in enumerate(blocks):

        @pl.when(flags[index] == 1)
        def _(operand=operand, start=start):
            key_ref, value_ref = others[2 * operand], others[2 * operand + 1]
            for g in range(group):
                cols = slice(g * DH, (g + 1) * DH)
                score = scores(q_ref[:, cols], key_ref[start : start + rows, cols])
                before = peak_ref[g][:, :1]
                peak = jnp.maximum(before, jnp.max(score, axis=-1, keepdims=True))
                weights = jnp.exp2(score - peak)
                factor = jnp.exp2(before - peak)
                total = total_ref[g][:, :1] * factor + jnp.sum(weights, axis=-1, keepdims=True)
                accum_ref[g] = accum_ref[g] * factor + jnp.dot(
                    weights.astype(jnp.bfloat16),
                    value_ref[start : start + rows, cols],
                    preferred_element_type=jnp.float32,
                )
                peak_ref[g] = jnp.broadcast_to(peak, (rows, LANES))
                total_ref[g] = jnp.broadcast_to(total, (rows, LANES))

    for g in range(group):
        cols = slice(g * DH, (g + 1) * DH)
        out_ref[:, cols] = (accum_ref[g] / total_ref[g][:, :1]).astype(jnp.bfloat16)


def self_attention(flags, queries, keys, values, others, blocks):
    rows, width = queries.shape
    heads = width // DH
    group = math.gcd(heads, 4)

    def spec(array):
        return pl.BlockSpec((array.shape[0], group * DH), lambda h, flags: (0, h))

    operands = [queries, keys, values] + [array for pair in others for array in pair]
    pairs = (len(blocks) + 1) * rows * rows * heads
    return pl.pallas_call(
        functools.partial(self_kernel, group=group, blocks=blocks, rows=rows),
        out_shape=jax.ShapeDtypeStruct((rows, width), jnp.bfloat16),
        grid_spec=pltpu.PrefetchScalarGridSpec(
            num_scalar_prefetch=1,
            grid=(heads // group,),
            in_specs=[spec(array) for array in operands],
            out_specs=spec(queries),
            scratch_shapes=[
                pltpu.VMEM((group, rows, LANES), jnp.float32),
                pltpu.VMEM((group, rows, LANES), jnp.float32),
                pltpu.VMEM((group, rows, DH), jnp.float32),
            ],
        ),
        compiler_params=pltpu.CompilerParams(vmem_limit_bytes=VMEM_BYTES),
        cost_estimate=pl.CostEstimate(
            flops=4 * pairs * DH,
            bytes_accessed=sum(array.size * 2 for array in operands) + rows * width * 2,
            transcendentals=pairs,
        ),
        name="self_attention",
    )(flags, *operands)


def case_kernel(chosen_ref, *refs, group, heads, cases, rows):
    array_refs, (out_ref, held, sems) = refs[:-3], refs[-3:]
    copies = [
        pltpu.make_async_copy(ref, held.at[i], sems.at[i]) for i, ref in enumerate(array_refs)
    ]

    def run(chosen):
        needed = [0, 1, 2] + [i for pair in chosen for i in (3 + 2 * pair, 4 + 2 * pair)]
        for i in needed:
            copies[i].start()
        for i in needed:
            copies[i].wait()
        row = lax.broadcasted_iota(jnp.int32, (rows, rows), 0)
        col = lax.broadcasted_iota(jnp.int32, (rows, rows), 1)
        pairs = [(1, 2)] + [(3 + 2 * pair, 4 + 2 * pair) for pair in chosen]

        @pl.loop(0, heads // group)
        def _(step):
            some = [
                pl.ds(pl.multiple_of((step * group + g) * DH, DH), DH) for g in range(group)
            ]
            found = [[scores(held[0, :, c], held[key, :, c]) for key, _ in pairs] for c in some]
            for score in found:
                score[0] = jnp.where(col <= row, score[0], NEG)
            peaks = [
                jnp.max(functools.reduce(jnp.maximum, score), axis=-1, keepdims=True)
                for score in found
            ]
            weights = [
                [jnp.exp2(part - peak).astype(jnp.bfloat16) for part in score]
                for score, peak in zip(found, peaks)
            ]
            for c, parts in zip(some, weights):
                both = sum(
                    jnp.dot(
                        part, with_ones(held[value, :, c]), preferred_element_type=jnp.float32
                    )
                    for part, (_, value) in zip(parts, pairs)
                )
                out_ref[:, c] = (both[:, :DH] / both[:, DH:]).astype(jnp.bfloat16)

    for index, chosen in enumerate(cases):
        pl.when(chosen_ref[0] == index)(functools.partial(run, chosen))


def self_attention_cases(chosen, queries, keys, values, others, cases):
    rows, width = queries.shape
    heads = width // DH
    operands = [queries, keys, values] + [array for pair in others for array in pair]
    pairs = (len(others) + 1) * rows * rows * heads
    return pl.pallas_call(
        functools.partial(
            case_kernel, group=math.gcd(heads, 4), heads=heads, cases=cases, rows=rows
        ),
        out_shape=jax.ShapeDtypeStruct((rows, width), jnp.bfloat16),
        in_specs=[pl.BlockSpec(memory_space=pltpu.SMEM)]
        + [pl.BlockSpec(memory_space=pltpu.HBM)] * len(operands),
        out_specs=pl.BlockSpec(memory_space=pltpu.VMEM),
        scratch_shapes=[
            pltpu.VMEM((len(operands), rows, width), jnp.bfloat16),
            pltpu.SemaphoreType.DMA((len(operands),)),
        ],
        compiler_params=pltpu.CompilerParams(vmem_limit_bytes=VMEM_BYTES),
        cost_estimate=pl.CostEstimate(
            flops=4 * pairs * DH,
            bytes_accessed=(len(operands) + 1) * rows * width * 2,
            transcendentals=pairs,
        ),
        name="self_attention",
    )(chosen, *operands)


def coded(value, heads, terms):
    total = 0.0
    for term in range(terms):
        rounded = value.astype(jnp.bfloat16).astype(jnp.float32)
        total = total + (pltpu.roll(rounded, term * heads, 1) if term else rounded)
        value = value - rounded
    return total.astype(jnp.bfloat16)


def local_kernel(meta, *refs, base, heads, span_count, near, queries):
    query_refs, refs = refs[:queries], refs[queries:]
    database_ref, out_ref, query, held, peak_ref, total_ref, accum_ref, sems, more = refs
    width = heads * DH
    rows = span_count * SPAN
    entries = span_count * near
    places = base + 2
    every = [slice(h * DH, (h + 1) * DH) for h in range(heads)]

    def fetch(entry, index):
        place = jnp.maximum(meta[places + entry], 0)
        return pltpu.make_async_copy(
            database_ref.at[index, place], held.at[index, entry], sems.at[index, entry]
        )

    picks = [pltpu.make_async_copy(ref, query, more) for ref in query_refs]
    for i, pick in enumerate(picks):
        pl.when(meta[base + i] == 1)(pick.start)
    for entry in range(entries):

        @pl.when(meta[places + entry] >= 0)
        def _(entry=entry):
            fetch(entry, 0).start()
            fetch(entry, 1).start()

    lane = lax.broadcasted_iota(jnp.int32, (1, LANES), 1)
    peak_ref[...] = jnp.full((rows, width), FLOOR, jnp.float32)
    total_ref[...] = jnp.zeros((rows, width), jnp.float32)
    accum_ref[...] = jnp.zeros((rows, width), jnp.float32)
    for i, pick in enumerate(picks):
        pl.when(meta[base + i] == 1)(pick.wait)

    @pl.loop(0, entries)
    def _(entry):
        @pl.when(meta[places + entry] >= 0)
        def _():
            fetch(entry, 0).wait()
            fetch(entry, 1).wait()
            here = pl.ds(pl.multiple_of((entry // near) * SPAN, SPAN), SPAN)
            found = [scores(query[here, c], held[0, entry, :, c]) for c in every]
            before = [peak_ref[here, c] for c in every]
            peaks = [
                jnp.maximum(old, jnp.max(score, axis=-1, keepdims=True))
                for old, score in zip(before, found)
            ]
            weights = [
                jnp.exp2(score - peak).astype(jnp.bfloat16) for score, peak in zip(found, peaks)
            ]
            factors = [jnp.exp2(old - peak) for old, peak in zip(before, peaks)]
            both = [
                jnp.dot(
                    weight, with_ones(held[1, entry, :, c]), preferred_element_type=jnp.float32
                )
                for weight, c in zip(weights, every)
            ]
            accums = [
                accum_ref[here, c] * factor + pair[:, :DH]
                for c, factor, pair in zip(every, factors, both)
            ]
            totals = [
                total_ref[here, c] * factor + pair[:, DH:]
                for c, factor, pair in zip(every, factors, both)
            ]
            for c, peak, accum, total in zip(every, peaks, accums, totals):
                peak_ref[here, c] = peak
                accum_ref[here, c] = accum
                total_ref[here, c] = total

    packed = jnp.zeros((rows, LANES), jnp.float32)
    for h, cols in enumerate(every):
        total = total_ref[:, cols]
        safe = jnp.where(total > 0.0, total, 1.0)
        out_ref[:, cols] = (accum_ref[:, cols] / safe).astype(jnp.bfloat16)
        level = jnp.where(total > 0.0, peak_ref[:, cols] + jnp.log2(safe), NEG)
        packed = jnp.where(lane == h, level, packed)
    out_ref[:, width:] = coded(packed, heads, 3)


def local_attention(meta, call, queries, database):
    rows, width = queries[0].shape
    heads = width // DH
    assert 3 * heads <= LANES
    span_count = rows // SPAN
    entries = meta.shape[1] - 2
    length = database.shape[2]
    pairs = rows * entries // span_count * length * heads // 4
    return pl.pallas_call(
        functools.partial(
            local_kernel,
            base=call * meta.shape[1],
            heads=heads,
            span_count=span_count,
            near=entries // span_count,
            queries=len(queries),
        ),
        out_shape=jax.ShapeDtypeStruct((rows, width + LANES), jnp.bfloat16),
        in_specs=[pl.BlockSpec(memory_space=pltpu.SMEM)]
        + [pl.BlockSpec(memory_space=pltpu.HBM)] * (len(queries) + 1),
        out_specs=pl.BlockSpec(memory_space=pltpu.VMEM),
        scratch_shapes=[
            pltpu.VMEM((rows, width), jnp.bfloat16),
            pltpu.VMEM((2, entries, length, width), jnp.bfloat16),
            pltpu.VMEM((rows, width), jnp.float32),
            pltpu.VMEM((rows, width), jnp.float32),
            pltpu.VMEM((rows, width), jnp.float32),
            pltpu.SemaphoreType.DMA((2, entries)),
            pltpu.SemaphoreType.DMA,
        ],
        compiler_params=pltpu.CompilerParams(vmem_limit_bytes=VMEM_BYTES),
        cost_estimate=pl.CostEstimate(
            flops=4 * pairs * DH,
            bytes_accessed=database.size // 2 + rows * width * 4,
            transcendentals=pairs,
        ),
        name="local_attention",
    )(meta.reshape(-1), *queries, database)


def merged(states, out_ref, heads, keep_level):
    width = heads * DH
    lane = lax.broadcasted_iota(jnp.int32, (1, LANES), 1)
    line = lax.broadcasted_iota(jnp.int32, (LANES, LANES), 0)
    levels = []
    for i in range(states.shape[0]):
        stats = states[i, :, width:].astype(jnp.float32)
        level = stats + pltpu.roll(stats, LANES - heads, 1)
        levels.append(level + pltpu.roll(stats, LANES - 2 * heads, 1))
    peak = functools.reduce(jnp.maximum, levels, jnp.full_like(levels[0], FLOOR))
    factors = [jnp.exp2(level - peak) for level in levels]
    total = functools.reduce(jnp.add, factors)
    safe = jnp.where(total > 0.0, total, 1.0)
    shares = [coded(jnp.where(lane < heads, factor / safe, 0.0), heads, 2) for factor in factors]
    for h in range(heads):
        cols = slice(h * DH, (h + 1) * DH)
        spread = ((line == h) | (line == heads + h)).astype(jnp.bfloat16)
        result = 0.0
        for i, share in enumerate(shares):
            scale = jnp.dot(share, spread, preferred_element_type=jnp.float32)
            result = result + scale * states[i, :, cols].astype(jnp.float32)
        out_ref[:, cols] = result.astype(jnp.bfloat16)
    if keep_level:
        level = jnp.where(total > 0.0, peak + jnp.log2(safe), NEG)
        out_ref[:, width:] = coded(jnp.where(lane < heads, level, 0.0), heads, 3)


def merge_kernel(active, *refs, heads):
    state_refs, (out_ref, states, sems) = refs[:-3], refs[-3:]

    @pl.when(active[0] == 1)
    def _():
        copies = [
            pltpu.make_async_copy(ref, states.at[i], sems.at[i]) for i, ref in enumerate(state_refs)
        ]
        for copy in copies:
            copy.start()
        for copy in copies:
            copy.wait()
        merged(states, out_ref, heads, True)


def merge(active, states):
    rows, wide = states[0].shape
    return pl.pallas_call(
        functools.partial(merge_kernel, heads=(wide - LANES) // DH),
        out_shape=jax.ShapeDtypeStruct((rows, wide), jnp.bfloat16),
        in_specs=[pl.BlockSpec(memory_space=pltpu.SMEM)]
        + [pl.BlockSpec(memory_space=pltpu.HBM)] * len(states),
        out_specs=pl.BlockSpec(memory_space=pltpu.VMEM),
        scratch_shapes=[
            pltpu.VMEM((len(states), rows, wide), jnp.bfloat16),
            pltpu.SemaphoreType.DMA((len(states),)),
        ],
        compiler_params=pltpu.CompilerParams(vmem_limit_bytes=VMEM_BYTES),
        cost_estimate=pl.CostEstimate(
            flops=2 * rows * wide * LANES * len(states),
            bytes_accessed=rows * wide * 2 * (len(states) + 1),
            transcendentals=0,
        ),
        name="merge",
    )(active[None], *states)


def project_kernel(meta, *refs, heads, count, sides, columns, tile):
    state_refs, refs = refs[:count], refs[count:]
    pieces = 1 + sum(len(side) for side in sides)
    weight_refs, (out_ref, states, x, held, sems, more) = refs[:pieces], refs[pieces:]
    lists = []
    taken = 1
    for side in sides:
        lists.append(
            [
                (ref, offset if isinstance(offset, int) else meta[offset[0]], size)
                for ref, (offset, size) in zip(weight_refs[taken : taken + len(side)], side)
            ]
        )
        taken += len(side)
    own = [(weight_refs[0], 0, weight_refs[0].shape[0])]
    steps = columns // tile

    def run(first, second):
        gets = [
            pltpu.make_async_copy(ref, states.at[i], more.at[i]) for i, ref in enumerate(state_refs)
        ]
        for get in gets:
            get.start()
        copies = []
        for slot, some in enumerate((first, second)):
            for n in range(steps):
                part = pl.ds(n * tile, tile)
                copies.append([])
                for index, (ref, offset, size) in enumerate(some):
                    if not isinstance(offset, int):
                        offset = pl.multiple_of(offset, size)
                    copy = pltpu.make_async_copy(
                        ref.at[:, part],
                        held.at[slot, pl.ds(offset, size), part],
                        sems.at[slot * steps + n, index],
                    )
                    copy.start()
                    copies[-1].append(copy)
        for get in gets:
            get.wait()
        merged(states, x, heads, False)
        for slot in range(2):
            for n in range(steps):
                for copy in copies[slot * steps + n]:
                    copy.wait()
                place = pl.multiple_of(meta[2 + slot] * columns + n * tile, tile)
                out_ref[:, pl.ds(place, tile)] = jnp.dot(
                    x[...],
                    held[slot, :, pl.ds(n * tile, tile)],
                    preferred_element_type=jnp.float32,
                ).astype(jnp.bfloat16)

    @pl.when((meta[0] == 1) & (meta[1] == 0))
    def _():
        run(own, lists[0])

    @pl.when((meta[0] == 1) & (meta[1] == 1))
    def _():
        run(lists[1], lists[2])


def project(meta, states, weight, sides):
    rows, wide = states[0].shape
    depth, columns = weight.shape
    operands = [weight] + [array for side in sides for array, _ in side]
    most = max(len(side) for side in sides)
    shapes = [[(offset, array.shape[0]) for array, offset in side] for side in sides]
    tile = math.gcd(columns, 1024)
    return pl.pallas_call(
        functools.partial(
            project_kernel,
            heads=depth // DH,
            count=len(states),
            sides=shapes,
            columns=columns,
            tile=tile,
        ),
        out_shape=jax.ShapeDtypeStruct((rows, 2 * columns), jnp.bfloat16),
        in_specs=[pl.BlockSpec(memory_space=pltpu.SMEM)]
        + [pl.BlockSpec(memory_space=pltpu.HBM)] * (len(states) + len(operands)),
        out_specs=pl.BlockSpec(memory_space=pltpu.VMEM),
        scratch_shapes=[
            pltpu.VMEM((len(states), rows, wide), jnp.bfloat16),
            pltpu.VMEM((rows, depth), jnp.bfloat16),
            pltpu.VMEM((2, depth, columns), jnp.bfloat16),
            pltpu.SemaphoreType.DMA((2 * (columns // tile), most)),
            pltpu.SemaphoreType.DMA((len(states),)),
        ],
        compiler_params=pltpu.CompilerParams(vmem_limit_bytes=VMEM_BYTES),
        cost_estimate=pl.CostEstimate(
            flops=4 * rows * depth * columns,
            bytes_accessed=4 * depth * columns + 2 * rows * (depth + 2 * columns),
            transcendentals=0,
        ),
        name="project",
    )(meta, *states, *operands)


def after(value, *earlier):
    return lax.optimization_barrier((value, *earlier))[0]


def shards(hidden_in, queries, keys, values, cross_queries, neighbours, database, out_weight):
    rows, width = queries.shape[1:]
    member_count = lax.axis_size("ctx")
    part_count = lax.axis_size("tp")
    assert lax.axis_size("db") == 4
    member = lax.axis_index("ctx")
    plane = lax.axis_index("db")
    part_index = lax.axis_index("tp")
    outer = (plane == 0) | (plane == 3)
    inner = jnp.logical_not(outer)
    two_level = member_count == 4
    CORE = [(0, 1), (1, 0), (2, 3), (3, 2)]
    ACROSS = [(0, 2), (1, 3), (2, 0), (3, 1)]

    def send(value, perm, axis="db"):
        return lax.ppermute(value, axis, perm)

    own_ids = neighbours[0].reshape(-1)
    ids = [own_ids] + [
        send(own_ids, [(i, (i + step) % 4) for i in range(4)]) for step in range(1, 4)
    ]
    per_owner = database.shape[1]
    stacked = jnp.stack(ids)
    local = jnp.where(stacked // per_owner == plane, stacked % per_owner, -1)
    seq_a = plane ^ 1
    seq_b = jnp.where(plane < 2, 2, 1)
    seq_c = jnp.where(plane < 2, 3, 0)
    is_outer = outer.astype(jnp.int32)
    is_inner = inner.astype(jnp.int32)

    def described(first, seq):
        head = jnp.stack([first, 1 - first]).astype(jnp.int32)
        return jnp.concatenate(
            [head, lax.dynamic_index_in_dim(local, (plane - seq) % 4, 0, keepdims=False)]
        )

    one = jnp.ones((), jnp.int32)
    zero = jnp.zeros((), jnp.int32)
    meta_own = jnp.concatenate(
        [
            jnp.stack([one, zero]),
            jnp.where(own_ids // per_owner == plane, own_ids % per_owner, -1),
        ]
    )[None]
    meta = jnp.stack(
        [
            described(one, seq_a),
            described(is_outer, seq_b),
            described(is_outer, seq_c),
        ]
    )

    def across(piece):
        return send(piece, ACROSS, "ctx") if two_level else piece

    def whole(piece, other):
        if not two_level:
            return [(lax.all_gather(piece, "ctx", axis=0, tiled=True), 0)]
        beside = send(piece, CORE, "ctx")
        corner = send(other, CORE, "ctx")
        return [(piece, (4,)), (other, (5,)), (beside, (6,)), (corner, (7,))]

    key, value = keys[0], values[0]
    query = cross_queries[0]
    query_a = send(query, PAIR)
    query_m = send(query, MIDDLE)
    depth = out_weight.shape[0]
    share = depth // member_count
    own_share = lax.dynamic_slice_in_dim(out_weight, member * share, share, axis=0)
    if two_level:
        key_y = send(key, [(0, 2), (1, 3)], "ctx")
    else:
        key_y = value_y = key
    local_own = local_attention(meta_own, 0, [query], database)

    query, query_a, query_m, own_share, local_own, meta = lax.optimization_barrier(
        (query, query_a, query_m, own_share, local_own, meta)
    )
    query_c = send(query_a, MIDDLE)
    query_b_out = send(query_m, OUTWARD)
    share_a = send(own_share, INWARD)
    if two_level:
        value_y = send(after(value, key_y, query_a), [(0, 2), (1, 3)], "ctx")
    local_a = local_attention(meta, 0, [query_a], database)
    local_b = local_attention(meta, 1, [query_b_out, after(query_m, local_a)], database)

    query_c, share_a, local_b, key_y, value_y = lax.optimization_barrier(
        (query_c, share_a, local_b, key_y, value_y)
    )
    query_c_out = send(query_c, OUTWARD)
    in_b = send(local_b, INWARD)
    share_b = send(after(own_share, query_c), MIDDLE)
    other_a = across(share_a)

    query_c_out, in_b, share_a, share_b, other_a, key, value, key_y, value_y = (
        lax.optimization_barrier(
            (query_c_out, in_b, share_a, share_b, other_a, key, value, key_y, value_y)
        )
    )
    local_c = local_attention(meta, 2, [query_c_out, query_c], database)
    in_c = send(local_c, INWARD)
    share_c = send(share_a, MIDDLE)
    other_b = across(share_b)
    pieces_a = whole(after(share_a, local_c), other_a)

    in_c, share_c, other_b, local_c = lax.optimization_barrier((in_c, share_c, other_b, local_c))
    merged_c = merge(is_inner, [local_c, in_c])
    mid_c = send(merged_c, MIDDLE)
    in_own = send(after(local_own, in_c), INWARD)
    merged_b = merge(is_inner, [after(local_b, merged_c), in_b])
    other_c = across(after(share_c, merged_b))
    mid_b = send(merged_b, MIDDLE)
    pieces_b = whole(after(share_b, merged_c), after(other_b, merged_c))
    mid_c, in_own, other_c = lax.optimization_barrier((mid_c, in_own, other_c, merged_b))[:3]
    pieces_c = whole(share_c, other_c)
    in_a = send(after(local_a, in_own), INWARD)

    side = plane // 2
    offsets = [member * share, (member ^ 2) * share, (member ^ 1) * share, (member ^ 3) * share]
    for_a = [local_a, in_own, mid_c]
    for_own = [local_own, in_a, mid_b]

    def projected(states, half):
        group = jnp.where(side == half, 0, 1)
        first = jnp.where(group == 0, plane % 2, seq_b % 2)
        second = jnp.where(group == 0, seq_a % 2, seq_c % 2)
        numbers = jnp.stack([is_inner, group, first, second, *offsets]).astype(jnp.int32)
        return project(numbers, states, out_weight, [pieces_a, pieces_b, pieces_c])

    def tied(states, *earlier):
        return [after(states[0], *earlier)] + states[1:]

    if part_count == 2:
        pair = [(0, 1), (1, 0)]
        mirrored = [(2 * a + t, 2 * b + 1 - t) for a, b in OUTWARD for t in range(2)]
        away_a = projected(for_a, 1 - part_index)
        first_a = lax.ppermute(away_a, ("db", "tp"), mirrored)
        kept_a = projected(tied(for_a, away_a), part_index)
        away = projected(tied(for_own, kept_a), 1 - part_index)
        first_own = send(away, pair, "tp")
        second_a = send(after(kept_a, first_a), OUTWARD)
        second_own = projected(tied(for_own, away), part_index)
        summed = jnp.where(outer, first_a, first_own).astype(jnp.float32) + jnp.where(
            outer, second_a, second_own
        ).astype(jnp.float32)
    else:
        away = merged_b

        def reduced(states):
            both = jnp.concatenate([projected(states, 0), projected(states, 1)], axis=1)
            return lax.psum_scatter(both, "tp", scatter_dimension=1, tiled=True)

        for_outer = send(reduced(for_a), OUTWARD)
        summed = jnp.where(outer, for_outer, reduced(for_own)).astype(jnp.float32)
    if two_level:
        beside = [(0, 1), (2, 3)]
        key, value, key_y, value_y = lax.optimization_barrier(
            (key, value, key_y, value_y, away)
        )[:4]
        key_c, value_c = send(key, beside, "ctx"), send(value, beside, "ctx")
        key_yc, value_yc = (
            send(key_y, [(2, 3), (3, 2)], "ctx"),
            send(value_y, [(2, 3), (3, 2)], "ctx"),
        )
        attended = self_attention_cases(
            member.astype(jnp.int32)[None],
            queries[0],
            key,
            value,
            [(key_c, value_c), (key_y, value_y), (key_yc, value_yc)],
            [[], [0], [1, 2], [0, 1, 2]],
        )
    else:
        key_all = lax.all_gather(key, "ctx", axis=0, tiled=True)
        value_all = lax.all_gather(value, "ctx", axis=0, tiled=True)
        blocks = [(0, j * rows) for j in range(member_count)]
        flags = (jnp.arange(member_count) < member).astype(jnp.int32)
        attended = self_attention(flags, queries[0], key, value, [(key_all, value_all)], blocks)
    mixed = (hidden_in[0].astype(jnp.float32) + summed).astype(jnp.bfloat16)
    return (attended[None], mixed[None])


def solution(mesh):
    in_specs = (
        P("db", "ctx", "tp"),
        P("db", "ctx", "tp"),
        P("db", "ctx", "tp"),
        P("db", "ctx", "tp"),
        P("db", "ctx", "tp"),
        P("db", "ctx", None),
        P(None, "db", None, "tp"),
        P("tp", "db"),
    )
    out_specs = (P("db", "ctx", "tp"), P("db", "ctx", "tp"))
    return jax.shard_map(shards, mesh=mesh, in_specs=in_specs, out_specs=out_specs, check_vma=False)
```

```python
import functools
import math

import jax
import jax.numpy as jnp
from jax import lax
from jax.experimental import pallas as pl
from jax.experimental.pallas import tpu as pltpu
from jax.sharding import PartitionSpec as P

DH = 128
PARTS = 1
SPAN = 64
LANES = 128
NEG = -1e30
FLOOR = -1e29
SCALE2 = math.log2(math.e) / math.sqrt(DH)
VMEM_BYTES = 48 * 1024 * 1024

PAIR = [(0, 1), (1, 0), (2, 3), (3, 2)]
MIDDLE = [(1, 2), (2, 1)]
INWARD = [(0, 1), (3, 2)]
OUTWARD = [(1, 0), (2, 3)]


def scores(query, key):
    return (
        lax.dot_general(query, key, (((1,), (1,)), ((), ())), preferred_element_type=jnp.float32)
        * SCALE2
    )


def with_ones(value):
    return jnp.concatenate([value, jnp.ones_like(value)], axis=1)


def self_kernel(flags, q_ref, k_ref, v_ref, *rest, group, blocks, rows):
    others, (out_ref, peak_ref, total_ref, accum_ref) = rest[:-4], rest[-4:]
    row = lax.broadcasted_iota(jnp.int32, (rows, rows), 0)
    col = lax.broadcasted_iota(jnp.int32, (rows, rows), 1)
    for g in range(group):
        cols = slice(g * DH, (g + 1) * DH)
        score = jnp.where(col <= row, scores(q_ref[:, cols], k_ref[:, cols]), NEG)
        peak = jnp.max(score, axis=-1, keepdims=True)
        weights = jnp.exp2(score - peak)
        total = jnp.sum(weights, axis=-1, keepdims=True)
        accum_ref[g] = jnp.dot(
            weights.astype(jnp.bfloat16), v_ref[:, cols], preferred_element_type=jnp.float32
        )
        peak_ref[g] = jnp.broadcast_to(peak, (rows, LANES))
        total_ref[g] = jnp.broadcast_to(total, (rows, LANES))
    for index, (operand, start) in enumerate(blocks):

        @pl.when(flags[index] == 1)
        def _(operand=operand, start=start):
            key_ref, value_ref = others[2 * operand], others[2 * operand + 1]
            for g in range(group):
                cols = slice(g * DH, (g + 1) * DH)
                score = scores(q_ref[:, cols], key_ref[start : start + rows, cols])
                before = peak_ref[g][:, :1]
                peak = jnp.maximum(before, jnp.max(score, axis=-1, keepdims=True))
                weights = jnp.exp2(score - peak)
                factor = jnp.exp2(before - peak)
                total = total_ref[g][:, :1] * factor + jnp.sum(weights, axis=-1, keepdims=True)
                accum_ref[g] = accum_ref[g] * factor + jnp.dot(
                    weights.astype(jnp.bfloat16),
                    value_ref[start : start + rows, cols],
                    preferred_element_type=jnp.float32,
                )
                peak_ref[g] = jnp.broadcast_to(peak, (rows, LANES))
                total_ref[g] = jnp.broadcast_to(total, (rows, LANES))

    for g in range(group):
        cols = slice(g * DH, (g + 1) * DH)
        out_ref[:, cols] = (accum_ref[g] / total_ref[g][:, :1]).astype(jnp.bfloat16)


def self_attention(flags, queries, keys, values, others, blocks):
    rows, width = queries.shape
    heads = width // DH
    group = math.gcd(heads, 4)

    def spec(array):
        return pl.BlockSpec((array.shape[0], group * DH), lambda h, flags: (0, h))

    operands = [queries, keys, values] + [array for pair in others for array in pair]
    pairs = (len(blocks) + 1) * rows * rows * heads
    return pl.pallas_call(
        functools.partial(self_kernel, group=group, blocks=blocks, rows=rows),
        out_shape=jax.ShapeDtypeStruct((rows, width), jnp.bfloat16),
        grid_spec=pltpu.PrefetchScalarGridSpec(
            num_scalar_prefetch=1,
            grid=(heads // group,),
            in_specs=[spec(array) for array in operands],
            out_specs=spec(queries),
            scratch_shapes=[
                pltpu.VMEM((group, rows, LANES), jnp.float32),
                pltpu.VMEM((group, rows, LANES), jnp.float32),
                pltpu.VMEM((group, rows, DH), jnp.float32),
            ],
        ),
        compiler_params=pltpu.CompilerParams(vmem_limit_bytes=VMEM_BYTES),
        cost_estimate=pl.CostEstimate(
            flops=4 * pairs * DH,
            bytes_accessed=sum(array.size * 2 for array in operands) + rows * width * 2,
            transcendentals=pairs,
        ),
        name="self_attention",
    )(flags, *operands)


def case_kernel(chosen_ref, *refs, group, heads, cases, rows):
    array_refs, (out_ref, held, sems) = refs[:-3], refs[-3:]
    copies = [
        pltpu.make_async_copy(ref, held.at[i], sems.at[i]) for i, ref in enumerate(array_refs)
    ]

    def run(chosen):
        needed = [0, 1, 2] + [i for pair in chosen for i in (3 + 2 * pair, 4 + 2 * pair)]
        for i in needed:
            copies[i].start()
        for i in needed:
            copies[i].wait()
        row = lax.broadcasted_iota(jnp.int32, (rows, rows), 0)
        col = lax.broadcasted_iota(jnp.int32, (rows, rows), 1)
        pairs = [(1, 2)] + [(3 + 2 * pair, 4 + 2 * pair) for pair in chosen]

        @pl.loop(0, heads // group)
        def _(step):
            some = [
                pl.ds(pl.multiple_of((step * group + g) * DH, DH), DH) for g in range(group)
            ]
            found = [[scores(held[0, :, c], held[key, :, c]) for key, _ in pairs] for c in some]
            for score in found:
                score[0] = jnp.where(col <= row, score[0], NEG)
            peaks = [
                jnp.max(functools.reduce(jnp.maximum, score), axis=-1, keepdims=True)
                for score in found
            ]
            weights = [
                [jnp.exp2(part - peak).astype(jnp.bfloat16) for part in score]
                for score, peak in zip(found, peaks)
            ]
            for c, parts in zip(some, weights):
                both = sum(
                    jnp.dot(
                        part, with_ones(held[value, :, c]), preferred_element_type=jnp.float32
                    )
                    for part, (_, value) in zip(parts, pairs)
                )
                out_ref[:, c] = (both[:, :DH] / both[:, DH:]).astype(jnp.bfloat16)

    for index, chosen in enumerate(cases):
        pl.when(chosen_ref[0] == index)(functools.partial(run, chosen))


def self_attention_cases(chosen, queries, keys, values, others, cases):
    rows, width = queries.shape
    heads = width // DH
    operands = [queries, keys, values] + [array for pair in others for array in pair]
    pairs = (len(others) + 1) * rows * rows * heads
    return pl.pallas_call(
        functools.partial(
            case_kernel, group=math.gcd(heads, 4), heads=heads, cases=cases, rows=rows
        ),
        out_shape=jax.ShapeDtypeStruct((rows, width), jnp.bfloat16),
        in_specs=[pl.BlockSpec(memory_space=pltpu.SMEM)]
        + [pl.BlockSpec(memory_space=pltpu.HBM)] * len(operands),
        out_specs=pl.BlockSpec(memory_space=pltpu.VMEM),
        scratch_shapes=[
            pltpu.VMEM((len(operands), rows, width), jnp.bfloat16),
            pltpu.SemaphoreType.DMA((len(operands),)),
        ],
        compiler_params=pltpu.CompilerParams(vmem_limit_bytes=VMEM_BYTES),
        cost_estimate=pl.CostEstimate(
            flops=4 * pairs * DH,
            bytes_accessed=(len(operands) + 1) * rows * width * 2,
            transcendentals=pairs,
        ),
        name="self_attention",
    )(chosen, *operands)


def coded(value, heads, terms):
    total = 0.0
    for term in range(terms):
        rounded = value.astype(jnp.bfloat16).astype(jnp.float32)
        total = total + (pltpu.roll(rounded, term * heads, 1) if term else rounded)
        value = value - rounded
    return total.astype(jnp.bfloat16)


def local_kernel(meta, *refs, base, heads, span_count, near, queries):
    query_refs, refs = refs[:queries], refs[queries:]
    database_ref, out_ref, query, held, peak_ref, total_ref, accum_ref, sems, more = refs
    width = heads * DH
    rows = span_count * SPAN
    entries = span_count * near
    places = base + 2
    every = [slice(h * DH, (h + 1) * DH) for h in range(heads)]

    def fetch(entry, index):
        place = jnp.maximum(meta[places + entry], 0)
        return pltpu.make_async_copy(
            database_ref.at[index, place], held.at[index, entry], sems.at[index, entry]
        )

    picks = [pltpu.make_async_copy(ref, query, more) for ref in query_refs]
    for i, pick in enumerate(picks):
        pl.when(meta[base + i] == 1)(pick.start)
    for entry in range(entries):

        @pl.when(meta[places + entry] >= 0)
        def _(entry=entry):
            fetch(entry, 0).start()
            fetch(entry, 1).start()

    lane = lax.broadcasted_iota(jnp.int32, (1, LANES), 1)
    peak_ref[...] = jnp.full((rows, width), FLOOR, jnp.float32)
    total_ref[...] = jnp.zeros((rows, width), jnp.float32)
    accum_ref[...] = jnp.zeros((rows, width), jnp.float32)
    for i, pick in enumerate(picks):
        pl.when(meta[base + i] == 1)(pick.wait)

    @pl.loop(0, entries)
    def _(entry):
        @pl.when(meta[places + entry] >= 0)
        def _():
            fetch(entry, 0).wait()
            fetch(entry, 1).wait()
            here = pl.ds(pl.multiple_of((entry // near) * SPAN, SPAN), SPAN)
            found = [scores(query[here, c], held[0, entry, :, c]) for c in every]
            before = [peak_ref[here, c] for c in every]
            peaks = [
                jnp.maximum(old, jnp.max(score, axis=-1, keepdims=True))
                for old, score in zip(before, found)
            ]
            weights = [
                jnp.exp2(score - peak).astype(jnp.bfloat16) for score, peak in zip(found, peaks)
            ]
            factors = [jnp.exp2(old - peak) for old, peak in zip(before, peaks)]
            both = [
                jnp.dot(
                    weight, with_ones(held[1, entry, :, c]), preferred_element_type=jnp.float32
                )
                for weight, c in zip(weights, every)
            ]
            accums = [
                accum_ref[here, c] * factor + pair[:, :DH]
                for c, factor, pair in zip(every, factors, both)
            ]
            totals = [
                total_ref[here, c] * factor + pair[:, DH:]
                for c, factor, pair in zip(every, factors, both)
            ]
            for c, peak, accum, total in zip(every, peaks, accums, totals):
                peak_ref[here, c] = peak
                accum_ref[here, c] = accum
                total_ref[here, c] = total

    packed = jnp.zeros((rows, LANES), jnp.float32)
    for h, cols in enumerate(every):
        total = total_ref[:, cols]
        safe = jnp.where(total > 0.0, total, 1.0)
        out_ref[:, cols] = (accum_ref[:, cols] / safe).astype(jnp.bfloat16)
        level = jnp.where(total > 0.0, peak_ref[:, cols] + jnp.log2(safe), NEG)
        packed = jnp.where(lane == h, level, packed)
    out_ref[:, width:] = coded(packed, heads, 3)


def local_attention(meta, call, queries, database):
    rows, width = queries[0].shape
    heads = width // DH
    assert 3 * heads <= LANES
    span_count = rows // SPAN
    entries = meta.shape[1] - 2
    length = database.shape[2]
    pairs = rows * entries // span_count * length * heads // 4
    return pl.pallas_call(
        functools.partial(
            local_kernel,
            base=call * meta.shape[1],
            heads=heads,
            span_count=span_count,
            near=entries // span_count,
            queries=len(queries),
        ),
        out_shape=jax.ShapeDtypeStruct((rows, width + LANES), jnp.bfloat16),
        in_specs=[pl.BlockSpec(memory_space=pltpu.SMEM)]
        + [pl.BlockSpec(memory_space=pltpu.HBM)] * (len(queries) + 1),
        out_specs=pl.BlockSpec(memory_space=pltpu.VMEM),
        scratch_shapes=[
            pltpu.VMEM((rows, width), jnp.bfloat16),
            pltpu.VMEM((2, entries, length, width), jnp.bfloat16),
            pltpu.VMEM((rows, width), jnp.float32),
            pltpu.VMEM((rows, width), jnp.float32),
            pltpu.VMEM((rows, width), jnp.float32),
            pltpu.SemaphoreType.DMA((2, entries)),
            pltpu.SemaphoreType.DMA,
        ],
        compiler_params=pltpu.CompilerParams(vmem_limit_bytes=VMEM_BYTES),
        cost_estimate=pl.CostEstimate(
            flops=4 * pairs * DH,
            bytes_accessed=database.size // 2 + rows * width * 4,
            transcendentals=pairs,
        ),
        name="local_attention",
    )(meta.reshape(-1), *queries, database)


def merged(states, out_ref, heads, keep_level):
    width = heads * DH
    lane = lax.broadcasted_iota(jnp.int32, (1, LANES), 1)
    line = lax.broadcasted_iota(jnp.int32, (LANES, LANES), 0)
    levels = []
    for i in range(states.shape[0]):
        stats = states[i, :, width:].astype(jnp.float32)
        level = stats + pltpu.roll(stats, LANES - heads, 1)
        levels.append(level + pltpu.roll(stats, LANES - 2 * heads, 1))
    peak = functools.reduce(jnp.maximum, levels, jnp.full_like(levels[0], FLOOR))
    factors = [jnp.exp2(level - peak) for level in levels]
    total = functools.reduce(jnp.add, factors)
    safe = jnp.where(total > 0.0, total, 1.0)
    shares = [coded(jnp.where(lane < heads, factor / safe, 0.0), heads, 2) for factor in factors]
    for h in range(heads):
        cols = slice(h * DH, (h + 1) * DH)
        spread = ((line == h) | (line == heads + h)).astype(jnp.bfloat16)
        result = 0.0
        for i, share in enumerate(shares):
            scale = jnp.dot(share, spread, preferred_element_type=jnp.float32)
            result = result + scale * states[i, :, cols].astype(jnp.float32)
        out_ref[:, cols] = result.astype(jnp.bfloat16)
    if keep_level:
        level = jnp.where(total > 0.0, peak + jnp.log2(safe), NEG)
        out_ref[:, width:] = coded(jnp.where(lane < heads, level, 0.0), heads, 3)


def merge_kernel(active, *refs, heads):
    state_refs, (out_ref, states, sems) = refs[:-3], refs[-3:]

    @pl.when(active[0] == 1)
    def _():
        copies = [
            pltpu.make_async_copy(ref, states.at[i], sems.at[i]) for i, ref in enumerate(state_refs)
        ]
        for copy in copies:
            copy.start()
        for copy in copies:
            copy.wait()
        merged(states, out_ref, heads, True)


def merge(active, states):
    rows, wide = states[0].shape
    return pl.pallas_call(
        functools.partial(merge_kernel, heads=(wide - LANES) // DH),
        out_shape=jax.ShapeDtypeStruct((rows, wide), jnp.bfloat16),
        in_specs=[pl.BlockSpec(memory_space=pltpu.SMEM)]
        + [pl.BlockSpec(memory_space=pltpu.HBM)] * len(states),
        out_specs=pl.BlockSpec(memory_space=pltpu.VMEM),
        scratch_shapes=[
            pltpu.VMEM((len(states), rows, wide), jnp.bfloat16),
            pltpu.SemaphoreType.DMA((len(states),)),
        ],
        compiler_params=pltpu.CompilerParams(vmem_limit_bytes=VMEM_BYTES),
        cost_estimate=pl.CostEstimate(
            flops=2 * rows * wide * LANES * len(states),
            bytes_accessed=rows * wide * 2 * (len(states) + 1),
            transcendentals=0,
        ),
        name="merge",
    )(active[None], *states)


def project_kernel(meta, *refs, heads, count, sides, columns, tile):
    state_refs, refs = refs[:count], refs[count:]
    pieces = 1 + sum(len(side) for side in sides)
    weight_refs, (out_ref, states, x, held, sems, more) = refs[:pieces], refs[pieces:]
    lists = []
    taken = 1
    for side in sides:
        lists.append(
            [
                (ref, offset if isinstance(offset, int) else meta[offset[0]], size)
                for ref, (offset, size) in zip(weight_refs[taken : taken + len(side)], side)
            ]
        )
        taken += len(side)
    own = [(weight_refs[0], 0, weight_refs[0].shape[0])]
    steps = columns // tile

    def run(first, second):
        gets = [
            pltpu.make_async_copy(ref, states.at[i], more.at[i]) for i, ref in enumerate(state_refs)
        ]
        for get in gets:
            get.start()
        copies = []
        for slot, some in enumerate((first, second)):
            for n in range(steps):
                part = pl.ds(n * tile, tile)
                copies.append([])
                for index, (ref, offset, size) in enumerate(some):
                    if not isinstance(offset, int):
                        offset = pl.multiple_of(offset, size)
                    copy = pltpu.make_async_copy(
                        ref.at[:, part],
                        held.at[slot, pl.ds(offset, size), part],
                        sems.at[slot * steps + n, index],
                    )
                    copy.start()
                    copies[-1].append(copy)
        for get in gets:
            get.wait()
        merged(states, x, heads, False)
        for slot in range(2):
            for n in range(steps):
                for copy in copies[slot * steps + n]:
                    copy.wait()
                place = pl.multiple_of(meta[2 + slot] * columns + n * tile, tile)
                out_ref[:, pl.ds(place, tile)] = jnp.dot(
                    x[...],
                    held[slot, :, pl.ds(n * tile, tile)],
                    preferred_element_type=jnp.float32,
                ).astype(jnp.bfloat16)

    @pl.when((meta[0] == 1) & (meta[1] == 0))
    def _():
        run(own, lists[0])

    @pl.when((meta[0] == 1) & (meta[1] == 1))
    def _():
        run(lists[1], lists[2])


def project(meta, states, weight, sides):
    rows, wide = states[0].shape
    depth, columns = weight.shape
    operands = [weight] + [array for side in sides for array, _ in side]
    most = max(len(side) for side in sides)
    shapes = [[(offset, array.shape[0]) for array, offset in side] for side in sides]
    tile = math.gcd(columns, 1024)
    return pl.pallas_call(
        functools.partial(
            project_kernel,
            heads=depth // DH,
            count=len(states),
            sides=shapes,
            columns=columns,
            tile=tile,
        ),
        out_shape=jax.ShapeDtypeStruct((rows, 2 * columns), jnp.bfloat16),
        in_specs=[pl.BlockSpec(memory_space=pltpu.SMEM)]
        + [pl.BlockSpec(memory_space=pltpu.HBM)] * (len(states) + len(operands)),
        out_specs=pl.BlockSpec(memory_space=pltpu.VMEM),
        scratch_shapes=[
            pltpu.VMEM((len(states), rows, wide), jnp.bfloat16),
            pltpu.VMEM((rows, depth), jnp.bfloat16),
            pltpu.VMEM((2, depth, columns), jnp.bfloat16),
            pltpu.SemaphoreType.DMA((2 * (columns // tile), most)),
            pltpu.SemaphoreType.DMA((len(states),)),
        ],
        compiler_params=pltpu.CompilerParams(vmem_limit_bytes=VMEM_BYTES),
        cost_estimate=pl.CostEstimate(
            flops=4 * rows * depth * columns,
            bytes_accessed=4 * depth * columns + 2 * rows * (depth + 2 * columns),
            transcendentals=0,
        ),
        name="project",
    )(meta, *states, *operands)


def after(value, *earlier):
    return lax.optimization_barrier((value, *earlier))[0]


def shards(hidden_in, queries, keys, values, cross_queries, neighbours, database, out_weight):
    rows, width = queries.shape[1:]
    member_count = lax.axis_size("ctx")
    part_count = lax.axis_size("tp")
    assert lax.axis_size("db") == 4
    member = lax.axis_index("ctx")
    plane = lax.axis_index("db")
    part_index = lax.axis_index("tp")
    outer = (plane == 0) | (plane == 3)
    inner = jnp.logical_not(outer)
    two_level = member_count == 4
    CORE = [(0, 1), (1, 0), (2, 3), (3, 2)]
    ACROSS = [(0, 2), (1, 3), (2, 0), (3, 1)]

    def send(value, perm, axis="db"):
        return lax.ppermute(value, axis, perm)

    own_ids = neighbours[0].reshape(-1)
    ids = [own_ids] + [
        send(own_ids, [(i, (i + step) % 4) for i in range(4)]) for step in range(1, 4)
    ]
    per_owner = database.shape[1]
    stacked = jnp.stack(ids)
    local = jnp.where(stacked // per_owner == plane, stacked % per_owner, -1)
    seq_a = plane ^ 1
    seq_b = jnp.where(plane < 2, 2, 1)
    seq_c = jnp.where(plane < 2, 3, 0)
    is_outer = outer.astype(jnp.int32)
    is_inner = inner.astype(jnp.int32)

    def described(first, seq):
        head = jnp.stack([first, 1 - first]).astype(jnp.int32)
        return jnp.concatenate(
            [head, lax.dynamic_index_in_dim(local, (plane - seq) % 4, 0, keepdims=False)]
        )

    one = jnp.ones((), jnp.int32)
    zero = jnp.zeros((), jnp.int32)
    meta_own = jnp.concatenate(
        [
            jnp.stack([one, zero]),
            jnp.where(own_ids // per_owner == plane, own_ids % per_owner, -1),
        ]
    )[None]
    meta = jnp.stack(
        [
            described(one, seq_a),
            described(is_outer, seq_b),
            described(is_outer, seq_c),
        ]
    )

    def across(piece):
        return send(piece, ACROSS, "ctx") if two_level else piece

    def whole(piece, other):
        if not two_level:
            return [(lax.all_gather(piece, "ctx", axis=0, tiled=True), 0)]
        beside = send(piece, CORE, "ctx")
        corner = send(other, CORE, "ctx")
        return [(piece, (4,)), (other, (5,)), (beside, (6,)), (corner, (7,))]

    key, value = keys[0], values[0]
    query = cross_queries[0]
    query_a = send(query, PAIR)
    query_m = send(query, MIDDLE)
    depth = out_weight.shape[0]
    share = depth // member_count
    own_share = lax.dynamic_slice_in_dim(out_weight, member * share, share, axis=0)
    if two_level:
        key_y = send(key, [(0, 2), (1, 3)], "ctx")
    else:
        key_y = value_y = key
    local_own = local_attention(meta_own, 0, [query], database)

    query, query_a, query_m, own_share, local_own, meta = lax.optimization_barrier(
        (query, query_a, query_m, own_share, local_own, meta)
    )
    query_c = send(query_a, MIDDLE)
    query_b_out = send(query_m, OUTWARD)
    share_a = send(own_share, INWARD)
    if two_level:
        value_y = send(after(value, key_y, query_a), [(0, 2), (1, 3)], "ctx")
    local_a = local_attention(meta, 0, [query_a], database)
    local_b = local_attention(meta, 1, [query_b_out, after(query_m, local_a)], database)

    query_c, share_a, local_b, key_y, value_y = lax.optimization_barrier(
        (query_c, share_a, local_b, key_y, value_y)
    )
    query_c_out = send(query_c, OUTWARD)
    in_b = send(local_b, INWARD)
    share_b = send(after(own_share, query_c), MIDDLE)
    other_a = across(share_a)

    query_c_out, in_b, share_a, share_b, other_a, key, value, key_y, value_y = (
        lax.optimization_barrier(
            (query_c_out, in_b, share_a, share_b, other_a, key, value, key_y, value_y)
        )
    )
    local_c = local_attention(meta, 2, [query_c_out, query_c], database)
    in_c = send(local_c, INWARD)
    share_c = send(share_a, MIDDLE)
    other_b = across(share_b)
    pieces_a = whole(after(share_a, local_c), other_a)

    def beside_keys(key, value, key_y, value_y, *earlier):
        beside = [(0, 1), (2, 3)]
        key, value, key_y, value_y = lax.optimization_barrier(
            (key, value, key_y, value_y, *earlier)
        )[:4]
        key_c, value_c = send(key, beside, "ctx"), send(value, beside, "ctx")
        key_yc, value_yc = (
            send(key_y, [(2, 3), (3, 2)], "ctx"),
            send(value_y, [(2, 3), (3, 2)], "ctx"),
        )
        return key_c, value_c, key_yc, value_yc, key_y, value_y

    moved = beside_keys(key, value, key_y, value_y, local_c) if two_level else (key,)

    in_c, share_c, other_b, local_c, *moved = lax.optimization_barrier(
        (in_c, share_c, other_b, local_c, *moved)
    )
    merged_c = merge(is_inner, [local_c, in_c])
    mid_c = send(merged_c, MIDDLE)
    in_own = send(after(local_own, in_c), INWARD)
    merged_b = merge(is_inner, [after(local_b, merged_c), in_b])
    other_c = across(after(share_c, merged_b))
    mid_b = send(merged_b, MIDDLE)
    pieces_b = whole(after(share_b, merged_c), after(other_b, merged_c))
    mid_c, in_own, other_c = lax.optimization_barrier((mid_c, in_own, other_c, merged_b))[:3]
    pieces_c = whole(share_c, other_c)
    in_a = send(after(local_a, in_own), INWARD)

    side = plane // 2
    offsets = [member * share, (member ^ 2) * share, (member ^ 1) * share, (member ^ 3) * share]
    for_a = [local_a, in_own, mid_c]
    for_own = [local_own, in_a, mid_b]

    def projected(states, half):
        group = jnp.where(side == half, 0, 1)
        first = jnp.where(group == 0, plane % 2, seq_b % 2)
        second = jnp.where(group == 0, seq_a % 2, seq_c % 2)
        numbers = jnp.stack([is_inner, group, first, second, *offsets]).astype(jnp.int32)
        return project(numbers, states, out_weight, [pieces_a, pieces_b, pieces_c])

    def tied(states, *earlier):
        return [after(states[0], *earlier)] + states[1:]

    if part_count == 2:
        pair = [(0, 1), (1, 0)]
        mirrored = [(2 * a + t, 2 * b + 1 - t) for a, b in OUTWARD for t in range(2)]
        half = out_weight.shape[1]
        away_a = projected(for_a, 1 - part_index)
        first_a = lax.ppermute(away_a[:, :half], ("db", "tp"), mirrored)
        beside_a = send(away_a[:, half:], pair, "tp")
        kept_a = projected(tied(for_a, away_a), part_index)
        away = projected(tied(for_own, kept_a), 1 - part_index)
        first_own = send(away, pair, "tp")
        second_a = send(after(kept_a, first_a)[:, :half], OUTWARD)
        both_a = kept_a[:, half:].astype(jnp.float32) + beside_a.astype(jnp.float32)
        both_a = send(after(both_a.astype(jnp.bfloat16), first_a), OUTWARD)
        second_own = projected(tied(for_own, away), part_index)
        for_outer = jnp.concatenate(
            [first_a.astype(jnp.float32) + second_a.astype(jnp.float32), both_a.astype(jnp.float32)],
            axis=1,
        )
        for_inner = first_own.astype(jnp.float32) + second_own.astype(jnp.float32)
        summed = jnp.where(outer, for_outer, for_inner)
    else:

        def reduced(states):
            both = jnp.concatenate([projected(states, 0), projected(states, 1)], axis=1)
            return lax.psum_scatter(both, "tp", scatter_dimension=1, tiled=True)

        for_outer = send(reduced(for_a), OUTWARD)
        summed = jnp.where(outer, for_outer, reduced(for_own)).astype(jnp.float32)
    if two_level:
        key_c, value_c, key_yc, value_yc, key_y, value_y = moved
        attended = self_attention_cases(
            member.astype(jnp.int32)[None],
            queries[0],
            key,
            value,
            [(key_c, value_c), (key_y, value_y), (key_yc, value_yc)],
            [[], [0], [1, 2], [0, 1, 2]],
        )
    else:
        key_all = lax.all_gather(key, "ctx", axis=0, tiled=True)
        value_all = lax.all_gather(value, "ctx", axis=0, tiled=True)
        blocks = [(0, j * rows) for j in range(member_count)]
        flags = (jnp.arange(member_count) < member).astype(jnp.int32)
        attended = self_attention(flags, queries[0], key, value, [(key_all, value_all)], blocks)
    mixed = (hidden_in[0].astype(jnp.float32) + summed).astype(jnp.bfloat16)
    return (attended[None], mixed[None])


def solution(mesh):
    in_specs = (
        P("db", "ctx", "tp"),
        P("db", "ctx", "tp"),
        P("db", "ctx", "tp"),
        P("db", "ctx", "tp"),
        P("db", "ctx", "tp"),
        P("db", "ctx", None),
        P(None, "db", None, "tp"),
        P("tp", "db"),
    )
    out_specs = (P("db", "ctx", "tp"), P("db", "ctx", "tp"))
    return jax.shard_map(shards, mesh=mesh, in_specs=in_specs, out_specs=out_specs, check_vma=False)
```

```python
import functools
import math

import jax
import jax.numpy as jnp
from jax import lax
from jax.experimental import pallas as pl
from jax.experimental.pallas import tpu as pltpu
from jax.sharding import PartitionSpec as P

DH = 128
PARTS = 1
SPAN = 64
LANES = 128
NEG = -1e30
FLOOR = -1e29
SCALE2 = math.log2(math.e) / math.sqrt(DH)
VMEM_BYTES = 48 * 1024 * 1024

PAIR = [(0, 1), (1, 0), (2, 3), (3, 2)]
MIDDLE = [(1, 2), (2, 1)]
INWARD = [(0, 1), (3, 2)]
OUTWARD = [(1, 0), (2, 3)]


def scores(query, key):
    return (
        lax.dot_general(query, key, (((1,), (1,)), ((), ())), preferred_element_type=jnp.float32)
        * SCALE2
    )


def with_ones(value):
    return jnp.concatenate([value, jnp.ones_like(value)], axis=1)


def self_kernel(flags, q_ref, k_ref, v_ref, *rest, group, blocks, rows):
    others, (out_ref, peak_ref, total_ref, accum_ref) = rest[:-4], rest[-4:]
    row = lax.broadcasted_iota(jnp.int32, (rows, rows), 0)
    col = lax.broadcasted_iota(jnp.int32, (rows, rows), 1)
    for g in range(group):
        cols = slice(g * DH, (g + 1) * DH)
        score = jnp.where(col <= row, scores(q_ref[:, cols], k_ref[:, cols]), NEG)
        peak = jnp.max(score, axis=-1, keepdims=True)
        weights = jnp.exp2(score - peak)
        total = jnp.sum(weights, axis=-1, keepdims=True)
        accum_ref[g] = jnp.dot(
            weights.astype(jnp.bfloat16), v_ref[:, cols], preferred_element_type=jnp.float32
        )
        peak_ref[g] = jnp.broadcast_to(peak, (rows, LANES))
        total_ref[g] = jnp.broadcast_to(total, (rows, LANES))
    for index, (operand, start) in enumerate(blocks):

        @pl.when(flags[index] == 1)
        def _(operand=operand, start=start):
            key_ref, value_ref = others[2 * operand], others[2 * operand + 1]
            for g in range(group):
                cols = slice(g * DH, (g + 1) * DH)
                score = scores(q_ref[:, cols], key_ref[start : start + rows, cols])
                before = peak_ref[g][:, :1]
                peak = jnp.maximum(before, jnp.max(score, axis=-1, keepdims=True))
                weights = jnp.exp2(score - peak)
                factor = jnp.exp2(before - peak)
                total = total_ref[g][:, :1] * factor + jnp.sum(weights, axis=-1, keepdims=True)
                accum_ref[g] = accum_ref[g] * factor + jnp.dot(
                    weights.astype(jnp.bfloat16),
                    value_ref[start : start + rows, cols],
                    preferred_element_type=jnp.float32,
                )
                peak_ref[g] = jnp.broadcast_to(peak, (rows, LANES))
                total_ref[g] = jnp.broadcast_to(total, (rows, LANES))

    for g in range(group):
        cols = slice(g * DH, (g + 1) * DH)
        out_ref[:, cols] = (accum_ref[g] / total_ref[g][:, :1]).astype(jnp.bfloat16)


def self_attention(flags, queries, keys, values, others, blocks):
    rows, width = queries.shape
    heads = width // DH
    group = math.gcd(heads, 4)

    def spec(array):
        return pl.BlockSpec((array.shape[0], group * DH), lambda h, flags: (0, h))

    operands = [queries, keys, values] + [array for pair in others for array in pair]
    pairs = (len(blocks) + 1) * rows * rows * heads
    return pl.pallas_call(
        functools.partial(self_kernel, group=group, blocks=blocks, rows=rows),
        out_shape=jax.ShapeDtypeStruct((rows, width), jnp.bfloat16),
        grid_spec=pltpu.PrefetchScalarGridSpec(
            num_scalar_prefetch=1,
            grid=(heads // group,),
            in_specs=[spec(array) for array in operands],
            out_specs=spec(queries),
            scratch_shapes=[
                pltpu.VMEM((group, rows, LANES), jnp.float32),
                pltpu.VMEM((group, rows, LANES), jnp.float32),
                pltpu.VMEM((group, rows, DH), jnp.float32),
            ],
        ),
        compiler_params=pltpu.CompilerParams(vmem_limit_bytes=VMEM_BYTES),
        cost_estimate=pl.CostEstimate(
            flops=4 * pairs * DH,
            bytes_accessed=sum(array.size * 2 for array in operands) + rows * width * 2,
            transcendentals=pairs,
        ),
        name="self_attention",
    )(flags, *operands)


def case_kernel(chosen_ref, *refs, group, heads, cases, rows):
    array_refs, (out_ref, held, sems) = refs[:-3], refs[-3:]
    copies = [
        pltpu.make_async_copy(ref, held.at[i], sems.at[i]) for i, ref in enumerate(array_refs)
    ]

    def run(chosen):
        needed = [0, 1, 2] + [i for pair in chosen for i in (3 + 2 * pair, 4 + 2 * pair)]
        for i in needed:
            copies[i].start()
        for i in needed:
            copies[i].wait()
        row = lax.broadcasted_iota(jnp.int32, (rows, rows), 0)
        col = lax.broadcasted_iota(jnp.int32, (rows, rows), 1)
        pairs = [(1, 2)] + [(3 + 2 * pair, 4 + 2 * pair) for pair in chosen]

        @pl.loop(0, heads // group)
        def _(step):
            some = [
                pl.ds(pl.multiple_of((step * group + g) * DH, DH), DH) for g in range(group)
            ]
            found = [[scores(held[0, :, c], held[key, :, c]) for key, _ in pairs] for c in some]
            for score in found:
                score[0] = jnp.where(col <= row, score[0], NEG)
            peaks = [
                jnp.max(functools.reduce(jnp.maximum, score), axis=-1, keepdims=True)
                for score in found
            ]
            weights = [
                [jnp.exp2(part - peak).astype(jnp.bfloat16) for part in score]
                for score, peak in zip(found, peaks)
            ]
            for c, parts in zip(some, weights):
                both = sum(
                    jnp.dot(
                        part, with_ones(held[value, :, c]), preferred_element_type=jnp.float32
                    )
                    for part, (_, value) in zip(parts, pairs)
                )
                out_ref[:, c] = (both[:, :DH] / both[:, DH:]).astype(jnp.bfloat16)

    for index, chosen in enumerate(cases):
        pl.when(chosen_ref[0] == index)(functools.partial(run, chosen))


def self_attention_cases(chosen, queries, keys, values, others, cases):
    rows, width = queries.shape
    heads = width // DH
    operands = [queries, keys, values] + [array for pair in others for array in pair]
    pairs = (len(others) + 1) * rows * rows * heads
    return pl.pallas_call(
        functools.partial(
            case_kernel, group=math.gcd(heads, 4), heads=heads, cases=cases, rows=rows
        ),
        out_shape=jax.ShapeDtypeStruct((rows, width), jnp.bfloat16),
        in_specs=[pl.BlockSpec(memory_space=pltpu.SMEM)]
        + [pl.BlockSpec(memory_space=pltpu.HBM)] * len(operands),
        out_specs=pl.BlockSpec(memory_space=pltpu.VMEM),
        scratch_shapes=[
            pltpu.VMEM((len(operands), rows, width), jnp.bfloat16),
            pltpu.SemaphoreType.DMA((len(operands),)),
        ],
        compiler_params=pltpu.CompilerParams(vmem_limit_bytes=VMEM_BYTES),
        cost_estimate=pl.CostEstimate(
            flops=4 * pairs * DH,
            bytes_accessed=(len(operands) + 1) * rows * width * 2,
            transcendentals=pairs,
        ),
        name="self_attention",
    )(chosen, *operands)


def coded(value, heads, terms):
    total = 0.0
    for term in range(terms):
        rounded = value.astype(jnp.bfloat16).astype(jnp.float32)
        total = total + (pltpu.roll(rounded, term * heads, 1) if term else rounded)
        value = value - rounded
    return total.astype(jnp.bfloat16)


def local_kernel(meta, *refs, base, heads, span_count, near, queries):
    query_refs, refs = refs[:queries], refs[queries:]
    database_ref, out_ref, query, held, peak_ref, total_ref, accum_ref, sems, more = refs
    width = heads * DH
    rows = span_count * SPAN
    entries = span_count * near
    places = base + 2
    every = [slice(h * DH, (h + 1) * DH) for h in range(heads)]

    def fetch(entry, index):
        place = jnp.maximum(meta[places + entry], 0)
        return pltpu.make_async_copy(
            database_ref.at[index, place], held.at[index, entry], sems.at[index, entry]
        )

    picks = [pltpu.make_async_copy(ref, query, more) for ref in query_refs]
    for i, pick in enumerate(picks):
        pl.when(meta[base + i] == 1)(pick.start)
    for entry in range(entries):

        @pl.when(meta[places + entry] >= 0)
        def _(entry=entry):
            fetch(entry, 0).start()
            fetch(entry, 1).start()

    lane = lax.broadcasted_iota(jnp.int32, (1, LANES), 1)
    peak_ref[...] = jnp.full((rows, width), FLOOR, jnp.float32)
    total_ref[...] = jnp.zeros((rows, width), jnp.float32)
    accum_ref[...] = jnp.zeros((rows, width), jnp.float32)
    for i, pick in enumerate(picks):
        pl.when(meta[base + i] == 1)(pick.wait)

    @pl.loop(0, entries)
    def _(entry):
        @pl.when(meta[places + entry] >= 0)
        def _():
            fetch(entry, 0).wait()
            fetch(entry, 1).wait()
            here = pl.ds(pl.multiple_of((entry // near) * SPAN, SPAN), SPAN)
            found = [scores(query[here, c], held[0, entry, :, c]) for c in every]
            before = [peak_ref[here, c] for c in every]
            peaks = [
                jnp.maximum(old, jnp.max(score, axis=-1, keepdims=True))
                for old, score in zip(before, found)
            ]
            weights = [
                jnp.exp2(score - peak).astype(jnp.bfloat16) for score, peak in zip(found, peaks)
            ]
            factors = [jnp.exp2(old - peak) for old, peak in zip(before, peaks)]
            both = [
                jnp.dot(
                    weight, with_ones(held[1, entry, :, c]), preferred_element_type=jnp.float32
                )
                for weight, c in zip(weights, every)
            ]
            accums = [
                accum_ref[here, c] * factor + pair[:, :DH]
                for c, factor, pair in zip(every, factors, both)
            ]
            totals = [
                total_ref[here, c] * factor + pair[:, DH:]
                for c, factor, pair in zip(every, factors, both)
            ]
            for c, peak, accum, total in zip(every, peaks, accums, totals):
                peak_ref[here, c] = peak
                accum_ref[here, c] = accum
                total_ref[here, c] = total

    packed = jnp.zeros((rows, LANES), jnp.float32)
    for h, cols in enumerate(every):
        total = total_ref[:, cols]
        safe = jnp.where(total > 0.0, total, 1.0)
        out_ref[:, cols] = (accum_ref[:, cols] / safe).astype(jnp.bfloat16)
        level = jnp.where(total > 0.0, peak_ref[:, cols] + jnp.log2(safe), NEG)
        packed = jnp.where(lane == h, level, packed)
    out_ref[:, width:] = coded(packed, heads, 3)


def local_attention(meta, call, queries, database):
    rows, width = queries[0].shape
    heads = width // DH
    assert 3 * heads <= LANES
    span_count = rows // SPAN
    entries = meta.shape[1] - 2
    length = database.shape[2]
    pairs = rows * entries // span_count * length * heads // 4
    return pl.pallas_call(
        functools.partial(
            local_kernel,
            base=call * meta.shape[1],
            heads=heads,
            span_count=span_count,
            near=entries // span_count,
            queries=len(queries),
        ),
        out_shape=jax.ShapeDtypeStruct((rows, width + LANES), jnp.bfloat16),
        in_specs=[pl.BlockSpec(memory_space=pltpu.SMEM)]
        + [pl.BlockSpec(memory_space=pltpu.HBM)] * (len(queries) + 1),
        out_specs=pl.BlockSpec(memory_space=pltpu.VMEM),
        scratch_shapes=[
            pltpu.VMEM((rows, width), jnp.bfloat16),
            pltpu.VMEM((2, entries, length, width), jnp.bfloat16),
            pltpu.VMEM((rows, width), jnp.float32),
            pltpu.VMEM((rows, width), jnp.float32),
            pltpu.VMEM((rows, width), jnp.float32),
            pltpu.SemaphoreType.DMA((2, entries)),
            pltpu.SemaphoreType.DMA,
        ],
        compiler_params=pltpu.CompilerParams(vmem_limit_bytes=VMEM_BYTES),
        cost_estimate=pl.CostEstimate(
            flops=4 * pairs * DH,
            bytes_accessed=database.size // 2 + rows * width * 4,
            transcendentals=pairs,
        ),
        name="local_attention",
    )(meta.reshape(-1), *queries, database)


def merged(states, out_ref, heads, keep_level):
    width = heads * DH
    lane = lax.broadcasted_iota(jnp.int32, (1, LANES), 1)
    line = lax.broadcasted_iota(jnp.int32, (LANES, LANES), 0)
    levels = []
    for i in range(states.shape[0]):
        stats = states[i, :, width:].astype(jnp.float32)
        level = stats + pltpu.roll(stats, LANES - heads, 1)
        levels.append(level + pltpu.roll(stats, LANES - 2 * heads, 1))
    peak = functools.reduce(jnp.maximum, levels, jnp.full_like(levels[0], FLOOR))
    factors = [jnp.exp2(level - peak) for level in levels]
    total = functools.reduce(jnp.add, factors)
    safe = jnp.where(total > 0.0, total, 1.0)
    shares = [coded(jnp.where(lane < heads, factor / safe, 0.0), heads, 2) for factor in factors]
    for h in range(heads):
        cols = slice(h * DH, (h + 1) * DH)
        spread = ((line == h) | (line == heads + h)).astype(jnp.bfloat16)
        result = 0.0
        for i, share in enumerate(shares):
            scale = jnp.dot(share, spread, preferred_element_type=jnp.float32)
            result = result + scale * states[i, :, cols].astype(jnp.float32)
        out_ref[:, cols] = result.astype(jnp.bfloat16)
    if keep_level:
        level = jnp.where(total > 0.0, peak + jnp.log2(safe), NEG)
        out_ref[:, width:] = coded(jnp.where(lane < heads, level, 0.0), heads, 3)


def merge_kernel(active, *refs, heads):
    state_refs, (out_ref, states, sems) = refs[:-3], refs[-3:]

    @pl.when(active[0] == 1)
    def _():
        copies = [
            pltpu.make_async_copy(ref, states.at[i], sems.at[i]) for i, ref in enumerate(state_refs)
        ]
        for copy in copies:
            copy.start()
        for copy in copies:
            copy.wait()
        merged(states, out_ref, heads, True)


def merge(active, states):
    rows, wide = states[0].shape
    return pl.pallas_call(
        functools.partial(merge_kernel, heads=(wide - LANES) // DH),
        out_shape=jax.ShapeDtypeStruct((rows, wide), jnp.bfloat16),
        in_specs=[pl.BlockSpec(memory_space=pltpu.SMEM)]
        + [pl.BlockSpec(memory_space=pltpu.HBM)] * len(states),
        out_specs=pl.BlockSpec(memory_space=pltpu.VMEM),
        scratch_shapes=[
            pltpu.VMEM((len(states), rows, wide), jnp.bfloat16),
            pltpu.SemaphoreType.DMA((len(states),)),
        ],
        compiler_params=pltpu.CompilerParams(vmem_limit_bytes=VMEM_BYTES),
        cost_estimate=pl.CostEstimate(
            flops=2 * rows * wide * LANES * len(states),
            bytes_accessed=rows * wide * 2 * (len(states) + 1),
            transcendentals=0,
        ),
        name="merge",
    )(active[None], *states)


def project_kernel(meta, *refs, heads, count, sides, columns, tile):
    state_refs, refs = refs[:count], refs[count:]
    pieces = 1 + sum(len(side) for side in sides)
    weight_refs, (out_ref, states, x, held, sems, more) = refs[:pieces], refs[pieces:]
    lists = []
    taken = 1
    for side in sides:
        lists.append(
            [
                (ref, offset if isinstance(offset, int) else meta[offset[0]], size)
                for ref, (offset, size) in zip(weight_refs[taken : taken + len(side)], side)
            ]
        )
        taken += len(side)
    own = [(weight_refs[0], 0, weight_refs[0].shape[0])]
    steps = columns // tile

    def run(first, second):
        gets = [
            pltpu.make_async_copy(ref, states.at[i], more.at[i]) for i, ref in enumerate(state_refs)
        ]
        for get in gets:
            get.start()
        copies = []
        for slot, some in enumerate((first, second)):
            for n in range(steps):
                part = pl.ds(n * tile, tile)
                copies.append([])
                for index, (ref, offset, size) in enumerate(some):
                    if not isinstance(offset, int):
                        offset = pl.multiple_of(offset, size)
                    copy = pltpu.make_async_copy(
                        ref.at[:, part],
                        held.at[slot, pl.ds(offset, size), part],
                        sems.at[slot * steps + n, index],
                    )
                    copy.start()
                    copies[-1].append(copy)
        for get in gets:
            get.wait()
        merged(states, x, heads, False)
        for slot in range(2):
            for n in range(steps):
                for copy in copies[slot * steps + n]:
                    copy.wait()
                place = pl.multiple_of(meta[2 + slot] * columns + n * tile, tile)
                out_ref[:, pl.ds(place, tile)] = jnp.dot(
                    x[...],
                    held[slot, :, pl.ds(n * tile, tile)],
                    preferred_element_type=jnp.float32,
                ).astype(jnp.bfloat16)

    @pl.when((meta[0] == 1) & (meta[1] == 0))
    def _():
        run(own, lists[0])

    @pl.when((meta[0] == 1) & (meta[1] == 1))
    def _():
        run(lists[1], lists[2])


def project(meta, states, weight, sides):
    rows, wide = states[0].shape
    depth, columns = weight.shape
    operands = [weight] + [array for side in sides for array, _ in side]
    most = max(len(side) for side in sides)
    shapes = [[(offset, array.shape[0]) for array, offset in side] for side in sides]
    tile = math.gcd(columns, 1024)
    return pl.pallas_call(
        functools.partial(
            project_kernel,
            heads=depth // DH,
            count=len(states),
            sides=shapes,
            columns=columns,
            tile=tile,
        ),
        out_shape=jax.ShapeDtypeStruct((rows, 2 * columns), jnp.bfloat16),
        in_specs=[pl.BlockSpec(memory_space=pltpu.SMEM)]
        + [pl.BlockSpec(memory_space=pltpu.HBM)] * (len(states) + len(operands)),
        out_specs=pl.BlockSpec(memory_space=pltpu.VMEM),
        scratch_shapes=[
            pltpu.VMEM((len(states), rows, wide), jnp.bfloat16),
            pltpu.VMEM((rows, depth), jnp.bfloat16),
            pltpu.VMEM((2, depth, columns), jnp.bfloat16),
            pltpu.SemaphoreType.DMA((2 * (columns // tile), most)),
            pltpu.SemaphoreType.DMA((len(states),)),
        ],
        compiler_params=pltpu.CompilerParams(vmem_limit_bytes=VMEM_BYTES),
        cost_estimate=pl.CostEstimate(
            flops=4 * rows * depth * columns,
            bytes_accessed=4 * depth * columns + 2 * rows * (depth + 2 * columns),
            transcendentals=0,
        ),
        name="project",
    )(meta, *states, *operands)


def after(value, *earlier):
    return lax.optimization_barrier((value, *earlier))[0]


def shards(hidden_in, queries, keys, values, cross_queries, neighbours, database, out_weight):
    rows, width = queries.shape[1:]
    member_count = lax.axis_size("ctx")
    part_count = lax.axis_size("tp")
    assert lax.axis_size("db") == 4
    member = lax.axis_index("ctx")
    plane = lax.axis_index("db")
    part_index = lax.axis_index("tp")
    outer = (plane == 0) | (plane == 3)
    inner = jnp.logical_not(outer)
    two_level = member_count == 4
    CORE = [(0, 1), (1, 0), (2, 3), (3, 2)]
    ACROSS = [(0, 2), (1, 3), (2, 0), (3, 1)]

    def send(value, perm, axis="db"):
        return lax.ppermute(value, axis, perm)

    own_ids = neighbours[0].reshape(-1)
    ids = [own_ids] + [
        send(own_ids, [(i, (i + step) % 4) for i in range(4)]) for step in range(1, 4)
    ]
    per_owner = database.shape[1]
    stacked = jnp.stack(ids)
    local = jnp.where(stacked // per_owner == plane, stacked % per_owner, -1)
    seq_a = plane ^ 1
    seq_b = jnp.where(plane < 2, 2, 1)
    seq_c = jnp.where(plane < 2, 3, 0)
    is_outer = outer.astype(jnp.int32)
    is_inner = inner.astype(jnp.int32)

    def described(first, seq):
        head = jnp.stack([first, 1 - first]).astype(jnp.int32)
        return jnp.concatenate(
            [head, lax.dynamic_index_in_dim(local, (plane - seq) % 4, 0, keepdims=False)]
        )

    one = jnp.ones((), jnp.int32)
    zero = jnp.zeros((), jnp.int32)
    meta_own = jnp.concatenate(
        [
            jnp.stack([one, zero]),
            jnp.where(own_ids // per_owner == plane, own_ids % per_owner, -1),
        ]
    )[None]
    meta = jnp.stack(
        [
            described(one, seq_a),
            described(is_outer, seq_b),
            described(is_outer, seq_c),
        ]
    )

    def across(piece):
        return send(piece, ACROSS, "ctx") if two_level else piece

    def whole(piece, other):
        if not two_level:
            return [(lax.all_gather(piece, "ctx", axis=0, tiled=True), 0)]
        beside = send(piece, CORE, "ctx")
        corner = send(other, CORE, "ctx")
        return [(piece, (4,)), (other, (5,)), (beside, (6,)), (corner, (7,))]

    key, value = keys[0], values[0]
    query = cross_queries[0]
    query_a = send(query, PAIR)
    query_m = send(query, MIDDLE)
    depth = out_weight.shape[0]
    share = depth // member_count
    own_share = lax.dynamic_slice_in_dim(out_weight, member * share, share, axis=0)
    if two_level:
        key_y = send(key, [(0, 2), (1, 3)], "ctx")
    else:
        key_y = value_y = key
    local_own = local_attention(meta_own, 0, [query], database)

    query, query_a, query_m, own_share, local_own, meta = lax.optimization_barrier(
        (query, query_a, query_m, own_share, local_own, meta)
    )
    query_c = send(query_a, MIDDLE)
    query_b_out = send(query_m, OUTWARD)
    share_a = send(own_share, INWARD)
    if two_level:
        value_y = send(after(value, key_y, query_a), [(0, 2), (1, 3)], "ctx")
    local_a = local_attention(meta, 0, [query_a], database)
    local_b = local_attention(meta, 1, [query_b_out, after(query_m, local_a)], database)

    query_c_out = send(after(query_c, query_b_out), OUTWARD)
    share_a, local_b, key_y, value_y = lax.optimization_barrier((share_a, local_b, key_y, value_y))
    in_b = send(local_b, INWARD)
    share_b = send(after(own_share, query_c), MIDDLE)
    other_a = across(share_a)

    query_c_out, in_b, share_a, share_b, other_a, key, value, key_y, value_y = (
        lax.optimization_barrier(
            (query_c_out, in_b, share_a, share_b, other_a, key, value, key_y, value_y)
        )
    )
    local_c = local_attention(meta, 2, [query_c_out, query_c], database)
    in_c = send(local_c, INWARD)
    share_c = send(share_a, MIDDLE)
    other_b = across(share_b)
    pieces_a = whole(after(share_a, local_c), other_a)

    in_c, share_c, other_b, local_c = lax.optimization_barrier((in_c, share_c, other_b, local_c))
    merged_c = merge(is_inner, [local_c, in_c])
    mid_c = send(merged_c, MIDDLE)
    in_own = send(after(local_own, in_c), INWARD)
    merged_b = merge(is_inner, [after(local_b, merged_c), in_b])
    other_c = across(after(share_c, merged_b))
    mid_b = send(merged_b, MIDDLE)
    pieces_b = whole(after(share_b, merged_c), after(other_b, merged_c))
    mid_c, in_own, other_c = lax.optimization_barrier((mid_c, in_own, other_c, merged_b))[:3]
    pieces_c = whole(share_c, other_c)
    in_a = send(after(local_a, in_own), INWARD)

    side = plane // 2
    offsets = [member * share, (member ^ 2) * share, (member ^ 1) * share, (member ^ 3) * share]
    for_a = [local_a, in_own, mid_c]
    for_own = [local_own, in_a, mid_b]

    def projected(states, half):
        group = jnp.where(side == half, 0, 1)
        first = jnp.where(group == 0, plane % 2, seq_b % 2)
        second = jnp.where(group == 0, seq_a % 2, seq_c % 2)
        numbers = jnp.stack([is_inner, group, first, second, *offsets]).astype(jnp.int32)
        return project(numbers, states, out_weight, [pieces_a, pieces_b, pieces_c])

    def tied(states, *earlier):
        return [after(states[0], *earlier)] + states[1:]

    if part_count == 2:
        pair = [(0, 1), (1, 0)]
        mirrored = [(2 * a + t, 2 * b + 1 - t) for a, b in OUTWARD for t in range(2)]
        away_a = projected(for_a, 1 - part_index)
        first_a = lax.ppermute(away_a, ("db", "tp"), mirrored)
        kept_a = projected(tied(for_a, away_a), part_index)
        away = projected(tied(for_own, kept_a), 1 - part_index)
        first_own = send(away, pair, "tp")
        second_a = send(after(kept_a, first_a), OUTWARD)
        second_own = projected(tied(for_own, away), part_index)
        summed = jnp.where(outer, first_a, first_own).astype(jnp.float32) + jnp.where(
            outer, second_a, second_own
        ).astype(jnp.float32)
    else:
        away = merged_b

        def reduced(states):
            both = jnp.concatenate([projected(states, 0), projected(states, 1)], axis=1)
            return lax.psum_scatter(both, "tp", scatter_dimension=1, tiled=True)

        for_outer = send(reduced(for_a), OUTWARD)
        summed = jnp.where(outer, for_outer, reduced(for_own)).astype(jnp.float32)
    if two_level:
        beside = [(0, 1), (2, 3)]
        key, value, key_y, value_y = lax.optimization_barrier(
            (key, value, key_y, value_y, away)
        )[:4]
        key_c, value_c = send(key, beside, "ctx"), send(value, beside, "ctx")
        key_yc, value_yc = (
            send(key_y, [(2, 3), (3, 2)], "ctx"),
            send(value_y, [(2, 3), (3, 2)], "ctx"),
        )
        attended = self_attention_cases(
            member.astype(jnp.int32)[None],
            queries[0],
            key,
            value,
            [(key_c, value_c), (key_y, value_y), (key_yc, value_yc)],
            [[], [0], [1, 2], [0, 1, 2]],
        )
    else:
        key_all = lax.all_gather(key, "ctx", axis=0, tiled=True)
        value_all = lax.all_gather(value, "ctx", axis=0, tiled=True)
        blocks = [(0, j * rows) for j in range(member_count)]
        flags = (jnp.arange(member_count) < member).astype(jnp.int32)
        attended = self_attention(flags, queries[0], key, value, [(key_all, value_all)], blocks)
    mixed = (hidden_in[0].astype(jnp.float32) + summed).astype(jnp.bfloat16)
    return (attended[None], mixed[None])


def solution(mesh):
    in_specs = (
        P("db", "ctx", "tp"),
        P("db", "ctx", "tp"),
        P("db", "ctx", "tp"),
        P("db", "ctx", "tp"),
        P("db", "ctx", "tp"),
        P("db", "ctx", None),
        P(None, "db", None, "tp"),
        P("tp", "db"),
    )
    out_specs = (P("db", "ctx", "tp"), P("db", "ctx", "tp"))
    return jax.shard_map(shards, mesh=mesh, in_specs=in_specs, out_specs=out_specs, check_vma=False)
```
